128 devices in a mesh: seq: 32 (over y, z, core), ch: 4 (over x).
Axes of the slice: x: 4, y: 4, z: 4, core: 2. Of those that a mesh axis runs over, the one named last changes fastest.
Arguments:
- query_gate: bfloat16 [16384, 8192], P('seq', 'ch'), may hold values from -100 to 100
- key_branch: bfloat16 [16384, 8192], P('seq', 'ch'), may hold values from -6 to 6
- value_branch: bfloat16 [16384, 8192], P('seq', 'ch'), may hold values from -6 to 6
- norm_gain: float32 [8192], P('ch'), may hold values from 0.5 to 1.5
- residues: float32 [512, 16], P('ch'), may hold values from -4 to 4
- decay_rate: float32 [512, 16], P('ch'), may hold values from 3.0517578e-06 to 0.0333333333
- doc_lengths: int32 [16], replicated, may hold values from 1 to 4096, 16384 in all
- cotangent: bfloat16 [16384, 8192], P('seq', 'ch'), may hold values from -6 to 6
Outputs:
- layer_out: bfloat16 [16384, 8192], P('seq', 'ch')
- grad_query: bfloat16 [16384, 8192], P('seq', 'ch')
- grad_key: bfloat16 [16384, 8192], P('seq', 'ch')
- grad_value: bfloat16 [16384, 8192], P('seq', 'ch')
The draws below stay inside these ranges and needn't reach their ends.
All inputs are finite; a program needn't handle non-finite values.
Results may differ from the reference program's by a relative error of at most 0.005.
Values may be sent and summed in bfloat16 or wider, within the bound.
No kernel may reach another device: no remote copies, remote signals or barrier semaphores. Data moves between devices by JAX's collectives and lax.ppermute only.
A program may use at most 192 MiB of HBM per device.

```python
import math
import jax
import jax.numpy as jnp
import numpy as np
from jax import lax

D = 8192
GROUP = 16
R = 16
DOCS = 16
TOKENS = 16384
GROUPS = 512


def draw_query_gate(key, part):
    key = jax.random.fold_in(key, 11)
    noise_key, column_key = jax.random.split(key, 2)
    channel_ramp = jnp.arange(D, dtype=jnp.float32) / (D - 1)
    column_scale = jnp.exp(jax.random.uniform(column_key, (D,), jnp.float32, 0.0, math.log(10.0)) * 0.5)
    base_draw = jnp.clip(jax.random.normal(noise_key, (TOKENS, D), jnp.float32), -4.0, 4.0)
    values = base_draw * (3.0 ** channel_ramp)[None, :] * column_scale[None, :]
    return values.astype(jnp.bfloat16)


def draw_decay_rate(key, part):
    key = jax.random.fold_in(key, 23)
    pick_key, slow_key, middle_key, fast_key = jax.random.split(key, 4)
    shape = (GROUPS, R)
    category = jax.random.uniform(pick_key, shape, jnp.float32)
    slow_rate = jnp.exp(jax.random.uniform(slow_key, shape, jnp.float32, math.log(0.05 / TOKENS), math.log(2.0 / TOKENS)))
    middle_rate = jnp.exp(jax.random.uniform(middle_key, shape, jnp.float32, math.log(2.0 / TOKENS), math.log(1.0 / 50)))
    fast_rate = jax.random.uniform(fast_key, shape, jnp.float32, 1.0 / 50, 1.0 / 30)
    slow_share = 0.5
    middle_share = 0.75
    picked = jnp.where(category < slow_share, slow_rate, jnp.where(category < middle_share, middle_rate, fast_rate))
    return picked.astype(jnp.float32)


def levels(key, dims, pieces, low, largest):
    gain = 1.0
    for position, shards_of in pieces:
        heights = jax.random.uniform(jax.random.fold_in(jax.random.fold_in(key, 6), position), (shards_of,), jnp.float32, low / len(pieces), largest / len(pieces))
        gain = gain * jnp.repeat(jnp.exp(heights), dims[position] // shards_of).reshape((-1,) + (1,) * (len(dims) - 1 - position))
    return gain


def profile(count, total, limit, skew):
    weights = [(1 << 20) // math.isqrt(standing ** skew) + 1 for standing in range(2, count + 1)]
    spare, holding = total - limit - (count - 1), [1] * (count - 1)
    while spare > 0:
        movable = [i for i in range(count - 1) if holding[i] < limit]
        pool, budget = sum([weights[i] for i in movable]), spare
        for i in movable:
            extra = min(limit - holding[i], max(1, budget * weights[i] // pool), spare)
            holding[i] = holding[i] + extra
            spare = spare - extra
    return np.array([limit] + holding)


def ragged_sizes(key, amount, total, reach, lean):
    if amount == 2:
        one = jax.random.randint(key, (), max(1, total - reach), min(reach, total - 1) + 1)
        return jnp.stack([one, total - one])
    sizes = jnp.asarray(profile(amount, total, reach, lean), jnp.int32)
    twos = (amount - 1) // 2
    giver, receiver = sizes[1:1 + 2 * twos:2], sizes[2:2 + 2 * twos:2]
    slack = jnp.minimum(giver - 1, reach - receiver)
    shifted = jax.random.randint(jax.random.fold_in(key, 1), (twos,), 0, 1 << 20) % (slack + 1)
    sizes = sizes.at[1:1 + 2 * twos:2].set(giver - shifted).at[2:2 + 2 * twos:2].set(receiver + shifted)
    return sizes[jax.random.permutation(jax.random.fold_in(key, 2), amount)]


def gaussian(key, dims, spread, bound, cuts=(), kind=jnp.bfloat16):
    values = spread * jax.random.normal(key, dims, jnp.float32)
    if cuts:
        values = values * levels(key, dims, cuts, -0.22, 0.18)
    return jnp.clip(values, -bound, bound).astype(kind)


def setup_inputs(seed: int = 0) -> dict:
    key_list = jax.random.split(jax.random.key(seed), 9)
    query_gate = draw_query_gate(jax.random.fold_in(key_list[8], 71), 0)
    key_branch = gaussian(key_list[1], (TOKENS, D), 1.0, 6.0, ((0, 32), (1, 4)))
    value_branch = gaussian(key_list[2], (TOKENS, D), 1.0, 6.0, ((0, 32), (1, 4)))
    norm_gain = jnp.clip(1.0 + 0.1 * jax.random.normal(key_list[3], (D,), jnp.float32), 0.5, 1.5)
    residues = gaussian(key_list[4], (GROUPS, R), 1.0, 4.0, ((0, 4),), jnp.float32)
    decay_rate = draw_decay_rate(jax.random.fold_in(key_list[8], 71), 0)
    doc_lengths = ragged_sizes(key_list[6], DOCS, TOKENS, TOKENS // 4, 2).astype(jnp.int32)
    cotangent = gaussian(key_list[7], (TOKENS, D), 1.0, 6.0, ((0, 32), (1, 4)))
    return dict(query_gate=query_gate, key_branch=key_branch, value_branch=value_branch, norm_gain=norm_gain, residues=residues, decay_rate=decay_rate, doc_lengths=doc_lengths, cotangent=cotangent)


def doc_index(places, doc_lengths):
    doc_ends = jnp.cumsum(doc_lengths).astype(jnp.int32)
    doc_starts = (doc_ends - doc_lengths).astype(jnp.int32)
    before_here = (doc_starts[None, :] <= places[:, None]).astype(jnp.int32)
    return (lax.optimization_barrier(jnp.sum(before_here, axis=1)) - 1).astype(jnp.int32)

def reference(query_gate, key_branch, value_branch, norm_gain, residues, decay_rate, doc_lengths, cotangent):
    product = (key_branch.astype(jnp.float32) * value_branch.astype(jnp.float32)).astype(jnp.bfloat16)
    product = lax.optimization_barrier(product).astype(jnp.float32)
    channel_rate = jnp.repeat(decay_rate.T, GROUP, axis=1)
    channel_res = jnp.repeat(residues.T, GROUP, axis=1)
    step_decay = jnp.exp(-channel_rate)
    places = jnp.arange(TOKENS, dtype=jnp.int32)
    doc_ids = doc_index(places, doc_lengths)
    prior_ids = doc_index((places - 1).astype(jnp.int32), doc_lengths)
    keep_prior = (doc_ids == prior_ids).astype(jnp.float32)
    keep_after = jnp.concatenate([keep_prior[1:], jnp.zeros((1,), jnp.float32)])

    def advance(carry_state, inputs):
        values, keep_flag = inputs
        carry_state = step_decay * carry_state * keep_flag + values[None, :]
        return (carry_state, lax.optimization_barrier(jnp.sum(channel_res * carry_state, axis=0)))
    start_state = jnp.zeros((R, D), jnp.float32)
    _, conv_rows = lax.scan(advance, start_state, (product, keep_prior))
    query_float = query_gate.astype(jnp.float32)
    gated_rows = query_float * conv_rows
    inv_rms = lax.rsqrt(lax.optimization_barrier(jnp.mean(gated_rows * gated_rows, axis=1, keepdims=True)) + 1e-06)
    normed = gated_rows * inv_rms
    layer_out = (normed * norm_gain[None, :]).astype(jnp.bfloat16)
    grad_normed = cotangent.astype(jnp.float32) * norm_gain[None, :]
    inner_mean = lax.optimization_barrier(jnp.mean(grad_normed * normed, axis=1, keepdims=True))
    grad_gated = inv_rms * (grad_normed - normed * inner_mean)
    grad_query = (grad_gated * conv_rows).astype(jnp.bfloat16)
    grad_conv = grad_gated * query_float
    _, grad_product = lax.scan(advance, start_state, (grad_conv, keep_after), reverse=True)
    grad_key = (grad_product * value_branch.astype(jnp.float32)).astype(jnp.bfloat16)
    grad_value = (grad_product * key_branch.astype(jnp.float32)).astype(jnp.bfloat16)
    return (layer_out, grad_query, grad_key, grad_value)
```

```python
import jax
import jax.numpy as jnp
from jax import lax
from jax.experimental import pallas as pl
from jax.experimental.pallas import tpu as pltpu
from jax.sharding import PartitionSpec as P

C = 64
W = 128
LB = 256
G = 16
R = 16
NG = W // G
REACH = 4096
EPS = 1e-6
f32, bf16 = jnp.float32, jnp.bfloat16
VLIM = 48 * 1024 * 1024


def doc_index(places, doc_lengths):
    doc_ends = jnp.cumsum(doc_lengths)
    doc_starts = doc_ends - doc_lengths
    before_here = (doc_starts[None, :] <= places[:, None]).astype(jnp.int32)
    return jnp.sum(before_here, axis=1) - 1


def dot(a, b):
    return jnp.dot(a, b, preferred_element_type=f32)


def lane_group(rows):
    return lax.broadcasted_iota(jnp.int32, (rows, W), 1) // G


def swap_blocks(parts):
    parts = list(parts)
    blk = lane_group(parts[0].shape[0])
    bit = 1
    while bit < NG:
        low = (blk & bit) == 0
        for m in range(NG):
            if not m & bit:
                a, b = parts[m], parts[m | bit]
                parts[m] = jnp.where(low, a, pltpu.roll(b, G * bit, 1))
                parts[m | bit] = jnp.where(low, pltpu.roll(a, W - G * bit, 1), b)
        bit *= 2
    return parts


def chunk_states(x, mask, et, decay, join_ref, order, emit):
    blk = lane_group(R)
    xm = x * mask
    state = jnp.zeros((R, W), f32)
    for m in order:
        emit(m, state)
        rows = xm[m * C : (m + 1) * C]
        full = dot(et, jnp.concatenate([rows, rows], axis=0))
        own = full[0:R]
        for g in range(1, NG):
            own = jnp.where(blk == g, full[g * R : (g + 1) * R], own)
        state = own + join_ref[0, m] * (decay * state)
    return state


def carried(entries, lag):
    rows = NG * R
    diag = (lax.broadcasted_iota(jnp.int32, (rows, W), 0) // R) == lane_group(rows)
    lag2 = jnp.concatenate([lag, lag], axis=1)
    out = []
    for e in entries:
        spread = jnp.where(diag, jnp.concatenate([e] * NG, axis=0), 0.0)
        hi = spread.astype(bf16)
        lo = (spread - hi.astype(f32)).astype(bf16)
        out.append(dot(lag2, jnp.concatenate([hi, lo], axis=0)))
    return out


def first_kernel(join_ref, k_ref, v_ref, mask_ref, et_ref, dc_ref, prod_ref, ent_ref, own_ref):
    chunks = k_ref.shape[0] // C
    for s in range(LB // W):
        at = slice(s * W, (s + 1) * W)
        x = (k_ref[:, at].astype(f32) * v_ref[:, at].astype(f32)).astype(bf16)
        prod_ref[:, at] = x

        def emit(m, state):
            ent_ref[m, :, at] = state

        end = chunk_states(x, mask_ref[...], et_ref[s * W : (s + 1) * W, :], dc_ref[:, at], join_ref, range(chunks), emit)
        own_ref[:, at] = end.astype(bf16)


def toeplitz_kernel(top_ref, x_ref, seg_ref, tap_ref, y_ref, z_ref, o_ref):
    seg = seg_ref[...]
    for s in range(LB // W):
        at = slice(s * W, (s + 1) * W)
        z = swap_blocks([x_ref[m * C : (m + 1) * C, at].astype(f32) for m in range(NG)])

        def matrix(g):
            taps = jnp.broadcast_to(tap_ref[s * NG + g : s * NG + g + 1, :], (C, W))
            return pltpu.roll(taps, 0, 1, stride=1, stride_axis=0)[:, :C].astype(bf16)

        for g in range(NG):
            z0 = jnp.where(seg == 0, z[g], 0.0).astype(bf16)
            z1 = jnp.where(seg == 1, z[g], 0.0).astype(bf16)
            y2 = dot(matrix(g), jnp.concatenate([z0, z1], axis=1))
            z_ref[g] = z[g]
            o_ref[g] = jnp.where(seg == 0, y2[:, :W], y2[:, W:])

        @pl.when(top_ref[0, 0] > 1)
        def _():
            def again(p, carry):
                for g in range(NG):
                    zp = jnp.where(seg == p, z_ref[g], 0.0).astype(bf16)
                    o_ref[g] = jnp.where(seg == p, dot(matrix(g), zp), o_ref[g])
                return carry

            lax.fori_loop(2, top_ref[0, 0] + 1, again, 0)

        y = swap_blocks([o_ref[g] for g in range(NG)])
        for m in range(NG):
            y_ref[m * C : (m + 1) * C, at] = y[m]


def entry_states(got, keep_ref, far, decay, join_ref, ent_ref, at, order):
    total = jnp.zeros((R, W), f32)
    for n in reversed(range(len(got))):
        total = keep_ref[0, n] * got[n][:, at].astype(f32) + far * total
    entries = []
    for m in order:
        entries.append(ent_ref[m, :, at] + total)
        total = join_ref[0, m] * (decay * total)
    return entries


def gate_kernel(join_ref, keep_ref, *refs):
    got, refs = refs[:8], refs[8:]
    y_ref, ent_ref, q_ref, c_ref, gain_ref, lag_ref, dc_ref, far_ref, same_ref, conv_ref, stat_ref, acc_ref = refs
    chunks = y_ref.shape[0] // C
    step = pl.program_id(0)

    @pl.when(step == 0)
    def _():
        acc_ref[...] = jnp.zeros_like(acc_ref)

    for s in range(LB // W):
        at = slice(s * W, (s + 1) * W)
        entries = entry_states(got, keep_ref, far_ref[:, at], dc_ref[:, at], join_ref, ent_ref, at, range(chunks))
        parts = carried(entries, lag_ref[:, at])
        for m in range(chunks):
            rows = slice(m * C, (m + 1) * C)
            conv = y_ref[rows, at] + same_ref[rows, :] * parts[m]
            conv_ref[rows, at] = conv
            gated = q_ref[rows, at].astype(f32) * conv
            acc_ref[rows, :W] += gated * gated
            acc_ref[rows, W:] += c_ref[rows, at].astype(f32) * gain_ref[:, at] * gated

    @pl.when(step == pl.num_programs(0) - 1)
    def _():
        row = lax.broadcasted_iota(jnp.int32, (8, 2 * W), 0)
        lane = lax.broadcasted_iota(jnp.int32, (8, 2 * W), 1)
        pick = (row == lane // W).astype(f32)
        stat_ref[...] = lax.dot_general(
            pick, acc_ref[...], (((1,), (1,)), ((), ())), precision=lax.Precision.HIGHEST, preferred_element_type=f32
        )


def grad_kernel(
    join_ref, conv_ref, q_ref, c_ref, gain_ref, inv_ref, mean_ref, mask_ref, et_ref, dc_ref,
    out_ref, gq_ref, gc_ref, ent_ref, own_ref,
):
    chunks = conv_ref.shape[0] // C
    inv, mean = inv_ref[...], mean_ref[...]
    for s in range(LB // W):
        at = slice(s * W, (s + 1) * W)
        conv = conv_ref[:, at]
        q = q_ref[:, at].astype(f32)
        gain = gain_ref[:, at]
        normed = q * conv * inv
        out_ref[:, at] = (normed * gain).astype(bf16)
        grad_gated = inv * (c_ref[:, at].astype(f32) * gain - normed * mean)
        gq_ref[:, at] = (grad_gated * conv).astype(bf16)
        x = (grad_gated * q).astype(bf16)
        gc_ref[:, at] = x

        def emit(m, state):
            ent_ref[m, :, at] = state

        order = list(reversed(range(chunks)))
        end = chunk_states(x, mask_ref[...], et_ref[s * W : (s + 1) * W, :], dc_ref[:, at], join_ref, order, emit)
        own_ref[:, at] = end.astype(bf16)


def last_kernel(join_ref, keep_ref, *refs):
    got, refs = refs[:8], refs[8:]
    y_ref, ent_ref, k_ref, v_ref, lag_ref, dc_ref, far_ref, same_ref, gk_ref, gv_ref = refs
    chunks = y_ref.shape[0] // C
    for s in range(LB // W):
        at = slice(s * W, (s + 1) * W)
        order = list(reversed(range(chunks)))
        entries = entry_states(got, keep_ref, far_ref[:, at], dc_ref[:, at], join_ref, ent_ref, at, order)
        parts = carried(entries, lag_ref[:, at])
        for n, m in enumerate(order):
            rows = slice(m * C, (m + 1) * C)
            grad = y_ref[rows, at] + same_ref[rows, :] * parts[n]
            gk_ref[rows, at] = (grad * v_ref[rows, at].astype(f32)).astype(bf16)
            gv_ref[rows, at] = (grad * k_ref[rows, at].astype(f32)).astype(bf16)


def split_hi_lo(x):
    hi = x.astype(bf16)
    return hi, (x - hi.astype(f32)).astype(bf16)


def local(query_gate, key_branch, value_branch, norm_gain, residues, decay_rate, doc_lengths, cotangent):
    rows, width = query_gate.shape
    chunks = rows // C
    groups = residues.shape[0]
    devices = lax.axis_size("seq")
    here = lax.axis_index("seq")
    total_width = width * lax.axis_size("ch")
    shifts = range(1, REACH // rows + 1)

    start = here * rows
    docs = doc_index(start - 1 + jnp.arange(rows + 2, dtype=jnp.int32), doc_lengths)
    inner = docs[1:-1].reshape(chunks, C)
    first, last = inner[:, 0], inner[:, -1]
    prior, after = docs[0 : rows : C], docs[C + 1 :: C]
    seg = inner - first[:, None]
    top = jnp.max(seg).reshape(1, 1)
    seg_lanes = jnp.repeat(seg.T, G, axis=1)

    def spread(flags, dtype):
        return jnp.broadcast_to(flags.reshape(rows, 1).astype(dtype), (rows, W))

    last_mask = spread(inner == last[:, None], bf16)
    first_mask = spread(inner == first[:, None], bf16)
    same_prior = spread(inner == prior[:, None], f32)
    same_after = spread(inner == after[:, None], f32)
    join_f = (last == prior).astype(f32).reshape(1, chunks)
    join_b = (first == after).astype(f32).reshape(1, chunks)
    step = jnp.arange(len(shifts), dtype=jnp.int32) + 1
    end_docs = doc_index((here - step + 1) * rows - 1, doc_lengths)
    keep_f = ((end_docs == docs[0]) & (here >= step)).astype(f32).reshape(1, -1)
    begin_docs = doc_index((here + step) * rows, doc_lengths)
    keep_b = ((begin_docs == docs[-1]) & (here + step < devices)).astype(f32).reshape(1, -1)

    flat_rate = decay_rate.reshape(groups * R)
    flat_res = residues.reshape(groups * R)
    place = jnp.arange(C, dtype=f32)
    et_b = jnp.exp(-flat_rate[:, None] * place[None, :])
    et_f = jnp.exp(-flat_rate[:, None] * (C - 1 - place)[None, :])
    et_f = jnp.concatenate(split_hi_lo(et_f), axis=1)
    et_b = jnp.concatenate(split_hi_lo(et_b), axis=1)
    lag_f = (flat_res[None, :] * jnp.exp(-flat_rate[None, :] * (place + 1.0)[:, None])).astype(bf16)
    lag_b = (flat_res[None, :] * jnp.exp(-flat_rate[None, :] * (C - place)[:, None])).astype(bf16)
    lane = jnp.arange(W)
    back = (W - lane) % W

    def taps(lags):
        h = jnp.sum(residues[:, :, None] * jnp.exp(-decay_rate[:, :, None] * lags.astype(f32)), axis=1)
        return jnp.where(lags < C, h, 0.0)

    tap_f, tap_b = taps(back), taps(lane)
    rate_lanes = jnp.repeat(decay_rate.T, G, axis=1)
    decay = jnp.exp(-rate_lanes * C)
    far = jnp.exp(-rate_lanes * rows)
    gain = norm_gain.reshape(1, width)

    grid = (width // LB,)
    wide = pl.BlockSpec((rows, LB), lambda i: (0, i))
    modes = pl.BlockSpec((R, LB), lambda i: (0, i))
    lagged = pl.BlockSpec((C, LB), lambda i: (0, i))
    table = pl.BlockSpec((LB // G * R, 2 * C), lambda i: (i, 0))
    tapped = pl.BlockSpec((LB // G, W), lambda i: (i, 0))
    entry = pl.BlockSpec((chunks, R, LB), lambda i: (0, 0, i))
    row1 = pl.BlockSpec((1, LB), lambda i: (0, i))
    whole = pl.BlockSpec((rows, W), lambda i: (0, 0))
    seg_spec = pl.BlockSpec((C, W), lambda i: (0, 0))
    small = pl.BlockSpec(memory_space=pltpu.SMEM)
    params = pltpu.CompilerParams(vmem_limit_bytes=VLIM, dimension_semantics=("arbitrary",))

    def shaped(dtype, *shape):
        return jax.ShapeDtypeStruct(shape, dtype)

    full16, full32 = shaped(bf16, rows, width), shaped(f32, rows, width)
    entries, ends = shaped(f32, chunks, R, width), shaped(bf16, R, width)

    def send(x, way):
        return [lax.ppermute(x, "seq", [(i, (i + way * n) % devices) for i in range(devices)]) for n in shifts]

    def toeplitz(x, tap):
        return pl.pallas_call(
            toeplitz_kernel, grid=grid, in_specs=[small, wide, seg_spec, tapped], out_specs=wide, out_shape=full32,
            scratch_shapes=[pltpu.VMEM((NG, C, W), f32), pltpu.VMEM((NG, C, W), f32)], compiler_params=params,
            cost_estimate=pl.CostEstimate(flops=2 * rows * width * 512, bytes_accessed=6 * rows * width, transcendentals=0),
        )(top, x, seg_lanes, tap)

    product, ent_f, own_f = pl.pallas_call(
        first_kernel, grid=grid, in_specs=[small, wide, wide, whole, table, modes], out_specs=[wide, entry, modes],
        out_shape=[full16, entries, ends], compiler_params=params,
    )(join_f, key_branch, value_branch, last_mask, et_f, decay)
    got_f = send(own_f, 1)
    y_f = toeplitz(product, tap_f)
    conv, stat = pl.pallas_call(
        gate_kernel, grid=grid,
        in_specs=[small, small] + [modes] * 8 + [wide, entry, wide, wide, row1, lagged, modes, modes, whole],
        out_specs=[wide, pl.BlockSpec((8, rows), lambda i: (0, 0))], out_shape=[full32, shaped(f32, 8, rows)],
        scratch_shapes=[pltpu.VMEM((rows, 2 * W), f32)], compiler_params=params,
    )(join_f, keep_f, *got_f, y_f, ent_f, query_gate, cotangent, gain, lag_f, decay, far, same_prior)
    stat = lax.psum(stat, "ch")
    inv = lax.rsqrt(stat[0] / total_width + EPS)
    mean = inv * stat[1] / total_width
    layer_out, grad_query, grad_conv, ent_b, own_b = pl.pallas_call(
        grad_kernel, grid=grid,
        in_specs=[small, wide, wide, wide, row1, whole, whole, whole, table, modes],
        out_specs=[wide, wide, wide, entry, modes], out_shape=[full16, full16, full16, entries, ends],
        compiler_params=params,
    )(join_b, conv, query_gate, cotangent, gain, spread(inv, f32), spread(mean, f32), first_mask, et_b, decay)
    got_b = send(own_b, -1)
    y_b = toeplitz(grad_conv, tap_b)
    grad_key, grad_value = pl.pallas_call(
        last_kernel, grid=grid,
        in_specs=[small, small] + [modes] * 8 + [wide, entry, wide, wide, lagged, modes, modes, whole],
        out_specs=[wide, wide], out_shape=[full16, full16], compiler_params=params,
    )(join_b, keep_b, *got_b, y_b, ent_b, key_branch, value_branch, lag_b, decay, far, same_after)
    return layer_out, grad_query, grad_key, grad_value


def solution(mesh):
    tokens = P("seq", "ch")
    placed = (tokens, tokens, tokens, P("ch"), P("ch", None), P("ch", None), P(), tokens)
    return jax.shard_map(local, mesh=mesh, in_specs=placed, out_specs=(tokens,) * 4, check_vma=False)
```

```python
import jax
import jax.numpy as jnp
from jax import lax
from jax.experimental import pallas as pl
from jax.experimental.pallas import tpu as pltpu
from jax.sharding import PartitionSpec as P

C = 64
W = 128
LB = 512
G = 16
R = 16
NG = W // G
DOCS = 16
REACH = 4096
DEPTH = C + 3 * R
EPS = 1e-6
f32, bf16, i32 = jnp.float32, jnp.bfloat16, jnp.int32
VLIM = 61 * 1024 * 1024


def dot(a, b):
    return jnp.dot(a, b, preferred_element_type=f32)


def iota(rows, axis):
    return lax.broadcasted_iota(i32, (rows, W), axis)


def turn(x, lanes):
    return pltpu.roll(x, lanes % W, 1)


def swap_blocks(parts):
    parts = list(parts)
    blk = iota(parts[0].shape[0], 1) // G
    bit = 1
    while bit < NG:
        low = (blk & bit) == 0
        for m in range(NG):
            if not m & bit:
                a, b = parts[m], parts[m | bit]
                parts[m] = jnp.where(low, a, turn(b, G * bit))
                parts[m | bit] = jnp.where(low, turn(a, -G * bit), b)
        bit *= 2
    return parts


def fan_out(x):
    blk = iota(x.shape[0], 1) // G
    parts, bit = [x], NG // 2
    while bit:
        low = (blk & bit) == 0
        parts = [
            y
            for x in parts
            for y in (jnp.where(low, x, turn(x, G * bit)), jnp.where(low, turn(x, -G * bit), x))
        ]
        bit //= 2
    return parts


def docs_at(places, len_ref):
    found, start = jnp.full(places.shape, -1, i32), i32(0)
    for n in range(DOCS):
        found += (places >= start).astype(i32)
        start += len_ref[n]
    return found


def chunk_places(here_ref, rows):
    return here_ref[0, 0] * (C * NG) + (iota(rows, 1) // G) * C


def state_masks(here_ref, len_ref, way):
    blk = iota(R, 1) // G
    base = chunk_places(here_ref, R)
    tokens = docs_at(chunk_places(here_ref, C) + iota(C, 0), len_ref)
    if way > 0:
        end, enter = C - 1, 0
        order = blk
    else:
        end, enter = 0, C - 1
        order = NG - 1 - blk
    ends = docs_at(chunk_places(here_ref, C) + end, len_ref)
    reach = (tokens == ends).astype(f32).astype(bf16)
    own = docs_at(base + end, len_ref)
    joins = []
    for n in (1, 2, 4):
        there = docs_at(base + end - way * n * C, len_ref)
        joins.append(((own == there) & (order >= n)).astype(f32))
    prior = docs_at(base + enter - way, len_ref)
    into = ((docs_at(base + enter, len_ref) == prior) & (order >= 1)).astype(f32)
    return reach, joins, into


def chunk_states(z, rate_ref, first_row, masks, way):
    reach, joins, into = masks
    lane = iota(R, 1).astype(f32)
    blk = iota(R, 1) // G
    away = (C - 1.0) - lane if way > 0 else lane
    entries, last = [], jnp.zeros((R, W), f32)
    for g in range(NG):
        rate = rate_ref[first_row + g * R : first_row + (g + 1) * R, :]
        fall = jnp.exp(-rate * away)[:, :C]
        hi = fall.astype(bf16)
        lo = (fall - hi.astype(f32)).astype(bf16)
        both = dot(jnp.concatenate([hi, lo], axis=0), z[g] * reach)
        state = both[:R] + both[R:]
        decay = jnp.exp(-rate * C)
        for n, join in zip((1, 2, 4), joins):
            state += (decay * join) * turn(state, way * n * G)
            decay *= decay
        entries.append(into * turn(state, way * G))
        end = NG - 1 if way > 0 else 0
        last = jnp.where(blk == g, turn(state, (g - end) * G), last)
    return entries, last


def first_kernel(here_ref, len_ref, k_ref, v_ref, rate_ref, z_ref, ent_ref, own_ref):
    masks = state_masks(here_ref, len_ref, 1)
    for s in range(LB // W):
        at = slice(s * W, (s + 1) * W)
        x = (k_ref[:, at].astype(f32) * v_ref[:, at].astype(f32)).astype(bf16).astype(f32)
        z = [part.astype(bf16) for part in swap_blocks([x[m * C : (m + 1) * C] for m in range(NG)])]
        entries, last = chunk_states(z, rate_ref, s * NG * R, masks, 1)
        for g in range(NG):
            n = s * NG + g
            z_ref[n * C : (n + 1) * C, :] = z[g]
            ent_ref[n * R : (n + 1) * R, :] = entries[g]
        own_ref[:, at] = last.astype(bf16)


def table_kernel(tapf_ref, tapb_ref, rate_ref, res_ref, lf_ref, lb_ref):
    lane, row = iota(C, 1), iota(C, 0).astype(f32)
    for g in range(LB // G):
        at = slice(g, g + 1)
        rate = jnp.broadcast_to(rate_ref[at, :], (C, W))
        res = jnp.broadcast_to(res_ref[at, :], (C, W))
        for tap_ref, out_ref, lag in ((tapf_ref, lf_ref, row + 1.0), (tapb_ref, lb_ref, C - row)):
            taps = jnp.broadcast_to(tap_ref[at, :], (C, W))
            square = pltpu.roll(taps, 0, 1, stride=1, stride_axis=0)
            carry = res * jnp.exp(-rate * lag)
            hi = carry.astype(bf16).astype(f32)
            carry = jnp.where(lane < C + 2 * R, hi, jnp.where(lane < DEPTH, carry - hi, 0.0))
            out_ref[g * C : (g + 1) * C, :] = jnp.where(lane < C, square, carry).astype(bf16)


def segments(here_ref, len_ref, way):
    first = chunk_places(here_ref, C)
    tokens = docs_at(first + iota(C, 0), len_ref)
    if way > 0:
        return tokens - docs_at(first, len_ref)
    return docs_at(first + (C - 1), len_ref) - tokens


def convolve(here_ref, len_ref, keep_ref, got, far_ref, rate_ref, z_ref, ent_ref, left_ref, o_ref, seg, s, way):
    at = slice(s * W, (s + 1) * W)
    total, far = jnp.zeros((R, W), f32), far_ref[:, at]
    for n in reversed(range(len(got))):
        total = keep_ref[0, n] * got[n][:, at].astype(f32) + far * total
    blk = iota(R, 1) // G
    base = chunk_places(here_ref, R)
    start = here_ref[0, 0] * (C * NG)
    if way > 0:
        order, edge, enter = blk, start - 1, 0
    else:
        order, edge, enter = NG - 1 - blk, start + C * NG, C - 1
    from_far = (docs_at(base + enter, len_ref) == docs_at(jnp.full((R, W), edge, i32), len_ref)).astype(f32)
    span = (order * C).astype(f32)
    m0, m1 = (seg == 0).astype(f32).astype(bf16), (seg == 1).astype(f32).astype(bf16)
    none = jnp.zeros((3 * R, W), bf16)
    for g, arrived in enumerate(fan_out(total)):
        n = s * NG + g
        rate = rate_ref[n * R : (n + 1) * R, :]
        entry = ent_ref[n * R : (n + 1) * R, :] + arrived * (jnp.exp(-rate * span) * from_far)
        hi = entry.astype(bf16)
        lo = (entry - hi.astype(f32)).astype(bf16)
        z = z_ref[n * C : (n + 1) * C, :]
        right = jnp.concatenate(
            [jnp.concatenate([z * m0, hi, lo, hi], axis=0), jnp.concatenate([z * m1, none], axis=0)], axis=1
        )
        y = dot(left_ref[n * C : (n + 1) * C, :DEPTH], right)
        o_ref[g] = jnp.where(seg == 0, y[:, :W], y[:, W:])

    top = jnp.max(seg)

    @pl.when(top > 1)
    def _():
        def again(p, carry):
            mask = (seg == p).astype(f32).astype(bf16)
            for g in range(NG):
                n = s * NG + g
                square = left_ref[n * C : (n + 1) * C, :C]
                o_ref[g] = jnp.where(seg == p, dot(square, z_ref[n * C : (n + 1) * C, :] * mask), o_ref[g])
            return carry

        lax.fori_loop(2, top + 1, again, 0)

    return swap_blocks([o_ref[g] for g in range(NG)])


def gate_kernel(here_ref, len_ref, keep_ref, *refs):
    got, refs = refs[:8], refs[8:]
    far_ref, rate_ref, z_ref, ent_ref, left_ref, q_ref, c_ref, gain_ref, conv_ref, stat_ref, acc_ref, o_ref = refs
    step = pl.program_id(0)

    @pl.when(step == 0)
    def _():
        acc_ref[...] = jnp.zeros_like(acc_ref)

    seg = segments(here_ref, len_ref, 1)
    for s in range(LB // W):
        at = slice(s * W, (s + 1) * W)
        parts = convolve(here_ref, len_ref, keep_ref, got, far_ref, rate_ref, z_ref, ent_ref, left_ref, o_ref, seg, s, 1)
        for m, conv in enumerate(parts):
            rows = slice(m * C, (m + 1) * C)
            conv_ref[rows, at] = conv
            gated = q_ref[rows, at].astype(f32) * conv
            acc_ref[rows, :W] += gated * gated
            acc_ref[rows, W:] += c_ref[rows, at].astype(f32) * gain_ref[:, at] * gated

    @pl.when(step == pl.num_programs(0) - 1)
    def _():
        row = lax.broadcasted_iota(i32, (8, 2 * W), 0)
        lane = lax.broadcasted_iota(i32, (8, 2 * W), 1)
        pick = (row == lane // W).astype(f32)
        stat_ref[...] = lax.dot_general(
            pick, acc_ref[...], (((1,), (1,)), ((), ())), precision=lax.Precision.HIGHEST, preferred_element_type=f32
        )


def grad_kernel(
    here_ref, len_ref, conv_ref, q_ref, c_ref, gain_ref, inv_ref, mean_ref, rate_ref, z_ref, ent_ref, own_ref
):
    masks = state_masks(here_ref, len_ref, -1)
    for s in range(LB // W):
        at = slice(s * W, (s + 1) * W)
        gain = gain_ref[:, at]
        parts = []
        for m in range(NG):
            rows = slice(m * C, (m + 1) * C)
            inv = inv_ref[rows, :]
            q = q_ref[rows, at].astype(f32)
            normed = q * conv_ref[rows, at] * inv
            parts.append(inv * (c_ref[rows, at].astype(f32) * gain - normed * mean_ref[rows, :]) * q)
        z = [part.astype(bf16) for part in swap_blocks(parts)]
        entries, last = chunk_states(z, rate_ref, s * NG * R, masks, -1)
        for g in range(NG):
            n = s * NG + g
            z_ref[n * C : (n + 1) * C, :] = z[g]
            ent_ref[n * R : (n + 1) * R, :] = entries[g]
        own_ref[:, at] = last.astype(bf16)


def out_kernel(conv_ref, q_ref, c_ref, gain_ref, inv_ref, mean_ref, out_ref, gq_ref):
    inv, mean = inv_ref[...], mean_ref[...]
    for s in range(LB // W):
        at = slice(s * W, (s + 1) * W)
        conv, gain = conv_ref[:, at], gain_ref[:, at]
        normed = q_ref[:, at].astype(f32) * conv * inv
        out_ref[:, at] = (normed * gain).astype(bf16)
        gq_ref[:, at] = (inv * (c_ref[:, at].astype(f32) * gain - normed * mean) * conv).astype(bf16)


def last_kernel(here_ref, len_ref, keep_ref, *refs):
    got, refs = refs[:8], refs[8:]
    far_ref, rate_ref, z_ref, ent_ref, left_ref, k_ref, v_ref, gk_ref, gv_ref, o_ref = refs
    seg = segments(here_ref, len_ref, -1)
    for s in range(LB // W):
        at = slice(s * W, (s + 1) * W)
        parts = convolve(here_ref, len_ref, keep_ref, got, far_ref, rate_ref, z_ref, ent_ref, left_ref, o_ref, seg, s, -1)
        for m, grad in enumerate(parts):
            rows = slice(m * C, (m + 1) * C)
            gk_ref[rows, at] = (grad * v_ref[rows, at].astype(f32)).astype(bf16)
            gv_ref[rows, at] = (grad * k_ref[rows, at].astype(f32)).astype(bf16)


def doc_index(places, doc_lengths):
    doc_ends = jnp.cumsum(doc_lengths)
    doc_starts = doc_ends - doc_lengths
    return jnp.sum((doc_starts[None, :] <= places[:, None]).astype(i32), axis=1) - 1


def local(query_gate, key_branch, value_branch, norm_gain, residues, decay_rate, doc_lengths, cotangent):
    rows, width = query_gate.shape
    groups = residues.shape[0]
    devices = lax.axis_size("seq")
    here = lax.axis_index("seq")
    total_width = width * lax.axis_size("ch")
    shifts = range(1, REACH // rows + 1)
    here_arr = here.astype(i32).reshape(1, 1)

    step = jnp.arange(len(shifts), dtype=i32) + 1
    places = jnp.concatenate([(here - step + 1) * rows - 1, (here + step) * rows])
    docs = doc_index(places, doc_lengths)
    back, ahead = docs[: len(shifts)], docs[len(shifts) :]
    keep_f = ((back == back[0]) & (here >= step)).astype(f32).reshape(1, -1)
    keep_b = ((ahead == ahead[0]) & (here + step < devices)).astype(f32).reshape(1, -1)

    rates = jnp.broadcast_to(decay_rate.reshape(groups * R, 1), (groups * R, W))
    lane = jnp.arange(W)

    def taps(lags):
        h = jnp.sum(residues[:, :, None] * jnp.exp(-decay_rate[:, :, None] * lags.astype(f32)), axis=1)
        return jnp.where(lags < C, h, 0.0)

    tap_f, tap_b = taps((W - lane) % W), taps(lane)
    rate_rep, res_rep = jnp.tile(decay_rate, (1, NG)), jnp.tile(residues, (1, NG))
    far = jnp.exp(-jnp.repeat(decay_rate.T, G, axis=1) * rows)
    gain = norm_gain.reshape(1, width)

    grid = (width // LB,)
    wide = pl.BlockSpec((rows, LB), lambda i: (0, i))
    modes = pl.BlockSpec((R, LB), lambda i: (0, i))
    stacked = pl.BlockSpec((LB // G * C, W), lambda i: (i, 0))
    states = pl.BlockSpec((LB // G * R, W), lambda i: (i, 0))
    tapped = pl.BlockSpec((LB // G, W), lambda i: (i, 0))
    row1 = pl.BlockSpec((1, LB), lambda i: (0, i))
    whole = pl.BlockSpec((rows, W), lambda i: (0, 0))
    small = pl.BlockSpec(memory_space=pltpu.SMEM)
    params = pltpu.CompilerParams(vmem_limit_bytes=VLIM, dimension_semantics=("arbitrary",))

    def shaped(dtype, *shape):
        return jax.ShapeDtypeStruct(shape, dtype)

    full16, full32 = shaped(bf16, rows, width), shaped(f32, rows, width)
    stack16 = shaped(bf16, groups * C, W)
    entries, ends = shaped(f32, groups * R, W), shaped(bf16, R, width)
    scratch = pltpu.VMEM((NG, C, W), f32)

    def send(x, way):
        return [lax.ppermute(x, "seq", [(i, (i + way * n) % devices) for i in range(devices)]) for n in shifts]

    def spread(column):
        return jnp.broadcast_to(column[:, None], (rows, W))

    z_f, ent_f, own_f = pl.pallas_call(
        first_kernel, grid=grid, in_specs=[small, small, wide, wide, states], out_specs=[stacked, states, modes],
        out_shape=[stack16, entries, ends], compiler_params=params, name="first",
    )(here_arr, doc_lengths, key_branch, value_branch, rates)
    got_f = send(own_f, 1)
    left_f, left_b = pl.pallas_call(
        table_kernel, grid=grid, in_specs=[tapped] * 4, out_specs=[stacked] * 2, out_shape=[stack16] * 2,
        compiler_params=params, name="tables",
        cost_estimate=pl.CostEstimate(flops=8 * rows * width, bytes_accessed=4 * rows * width, transcendentals=0),
    )(tap_f, tap_b, rate_rep, res_rep)
    conv, stat = pl.pallas_call(
        gate_kernel, grid=grid,
        in_specs=[small] * 3 + [modes] * 9 + [states, stacked, states, stacked, wide, wide, row1],
        out_specs=[wide, pl.BlockSpec((8, rows), lambda i: (0, 0))], out_shape=[full32, shaped(f32, 8, rows)],
        scratch_shapes=[pltpu.VMEM((rows, 2 * W), f32), scratch], compiler_params=params, name="gate",
    )(here_arr, doc_lengths, keep_f, *got_f, far, rates, z_f, ent_f, left_f, query_gate, cotangent, gain)
    stat = lax.psum(stat, "ch")
    inv = lax.rsqrt(stat[0] / total_width + EPS)
    mean = inv * stat[1] / total_width
    inv, mean = spread(inv), spread(mean)
    z_b, ent_b, own_b = pl.pallas_call(
        grad_kernel, grid=grid, in_specs=[small, small, wide, wide, wide, row1, whole, whole, states],
        out_specs=[stacked, states, modes], out_shape=[stack16, entries, ends], compiler_params=params, name="grad",
    )(here_arr, doc_lengths, conv, query_gate, cotangent, gain, inv, mean, rates)
    got_b = send(own_b, -1)
    layer_out, grad_query = pl.pallas_call(
        out_kernel, grid=grid, in_specs=[wide, wide, wide, row1, whole, whole],
        out_specs=[wide, wide], out_shape=[full16, full16], compiler_params=params, name="outputs",
        cost_estimate=pl.CostEstimate(flops=8 * rows * width, bytes_accessed=12 * rows * width, transcendentals=0),
    )(conv, query_gate, cotangent, gain, inv, mean)
    grad_key, grad_value = pl.pallas_call(
        last_kernel, grid=grid,
        in_specs=[small] * 3 + [modes] * 9 + [states, stacked, states, stacked, wide, wide],
        out_specs=[wide, wide], out_shape=[full16, full16], scratch_shapes=[scratch], compiler_params=params, name="last",
    )(here_arr, doc_lengths, keep_b, *got_b, far, rates, z_b, ent_b, left_b, key_branch, value_branch)
    return layer_out, grad_query, grad_key, grad_value


def solution(mesh):
    tokens = P("seq", "ch")
    placed = (tokens, tokens, tokens, P("ch"), P("ch", None), P("ch", None), P(), tokens)
    return jax.shard_map(local, mesh=mesh, in_specs=placed, out_specs=(tokens,) * 4, check_vma=False)
```

```python
import functools

import jax
import jax.numpy as jnp
from jax import lax
from jax.experimental import pallas as pl
from jax.experimental.pallas import tpu as pltpu
from jax.sharding import PartitionSpec as P

C = 64
W = 128
LB = 512
G = 16
R = 16
NG = W // G
DOCS = 16
REACH = 4096
HOP = 4
DEPTH = C + 3 * R
EPS = 1e-6
f32, bf16, i32 = jnp.float32, jnp.bfloat16, jnp.int32
VLIM = 61 * 1024 * 1024


def dot(a, b):
    return jnp.dot(a, b, preferred_element_type=f32)


def iota(rows, axis):
    return lax.broadcasted_iota(i32, (rows, W), axis)


def turn(x, lanes):
    return pltpu.roll(x, lanes % W, 1)


def swap_blocks(parts):
    parts = list(parts)
    blk = iota(parts[0].shape[0], 1) // G
    bit = 1
    while bit < NG:
        low = (blk & bit) == 0
        for m in range(NG):
            if not m & bit:
                a, b = parts[m], parts[m | bit]
                parts[m] = jnp.where(low, a, turn(b, G * bit))
                parts[m | bit] = jnp.where(low, turn(a, -G * bit), b)
        bit *= 2
    return parts


def fan_out(x):
    blk = iota(x.shape[0], 1) // G
    parts, bit = [x], NG // 2
    while bit:
        low = (blk & bit) == 0
        parts = [
            y
            for x in parts
            for y in (jnp.where(low, x, turn(x, G * bit)), jnp.where(low, turn(x, -G * bit), x))
        ]
        bit //= 2
    return parts


def docs_at(places, len_ref):
    found, start = jnp.full(places.shape, -1, i32), i32(0)
    for n in range(DOCS):
        found += (places >= start).astype(i32)
        start += len_ref[n]
    return found


def chunk_places(here_ref, rows):
    return here_ref[0, 0] * (C * NG) + (iota(rows, 1) // G) * C


def spread_rates(rate_ref, rate_out_ref):
    groups = rate_ref.shape[0]
    width = rate_out_ref.shape[1]
    row = lax.broadcasted_iota(i32, (groups, width), 0)
    lane = lax.broadcasted_iota(i32, (groups, width), 1)
    pick = (row == (pl.program_id(0) * width + lane) // G).astype(f32)
    rate_out_ref[...] = lax.dot_general(
        rate_ref[...], pick, (((0,), (0,)), ((), ())), precision=lax.Precision.HIGHEST, preferred_element_type=f32
    )


def put_masks(here_ref, len_ref, reach_ref, join_ref, way):
    @pl.when(pl.program_id(0) == 0)
    def _():
        reach, joins, into = state_masks(here_ref, len_ref, way)
        reach_ref[...] = reach
        for n, join in enumerate(joins + [into]):
            join_ref[n] = join

    return reach_ref[...], [join_ref[n] for n in range(3)], join_ref[3]


def state_masks(here_ref, len_ref, way):
    blk = iota(R, 1) // G
    base = chunk_places(here_ref, R)
    tokens = docs_at(chunk_places(here_ref, C) + iota(C, 0), len_ref)
    if way > 0:
        end, enter = C - 1, 0
        order = blk
    else:
        end, enter = 0, C - 1
        order = NG - 1 - blk
    ends = docs_at(chunk_places(here_ref, C) + end, len_ref)
    reach = (tokens == ends).astype(f32).astype(bf16)
    own = docs_at(base + end, len_ref)
    joins = []
    for n in (1, 2, 4):
        there = docs_at(base + end - way * n * C, len_ref)
        joins.append(((own == there) & (order >= n)).astype(f32))
    prior = docs_at(base + enter - way, len_ref)
    into = ((docs_at(base + enter, len_ref) == prior) & (order >= 1)).astype(f32)
    return reach, joins, into


def chunk_states(z_ref, rates, masks, way):
    reach, joins, into = masks
    passes = LB // W
    lane = iota(R, 1).astype(f32)
    blk = iota(R, 1) // G
    away = (C - 1.0) - lane if way > 0 else lane
    rows = jnp.concatenate([rates[:, s * W : (s + 1) * W] for s in range(passes)], axis=0)
    spread = fan_out(rows)
    order = [(s, g) for s in range(passes) for g in range(NG)]
    rate = jnp.concatenate([spread[g][s * R : (s + 1) * R] for s, g in order], axis=0)
    fall = jnp.exp(-rate * jnp.concatenate([away] * len(order), axis=0))[:, :C]
    hi = fall.astype(bf16)
    lo = (fall - hi.astype(f32)).astype(bf16)
    states = []
    for n in range(len(order)):
        at = slice(n * R, (n + 1) * R)
        both = dot(jnp.concatenate([hi[at], lo[at]], axis=0), z_ref[n * C : (n + 1) * C, :] * reach)
        states.append(both[:R] + both[R:])
    decay = jnp.exp(-rate * C)
    for n, join in zip((1, 2, 4), joins):
        scales = [decay[k * R : (k + 1) * R] * join for k in range(len(order))]
        states = [x + scale * turn(x, way * n * G) for x, scale in zip(states, scales)]
        decay *= decay
    entries = [into * turn(x, way * G) for x in states]
    end = NG - 1 if way > 0 else 0
    last = []
    for s in range(passes):
        row = jnp.zeros((R, W), f32)
        for g in range(NG):
            row = jnp.where(blk == g, turn(states[s * NG + g], (g - end) * G), row)
        last.append(row)
    return entries, last


def put_states(z_ref, ent_ref, own_ref, rates, masks, way):
    entries, last = chunk_states(z_ref, rates, masks, way)
    for n, entry in enumerate(entries):
        ent_ref[n * R : (n + 1) * R, :] = entry
    for s, row in enumerate(last):
        own_ref[:, s * W : (s + 1) * W] = row.astype(bf16)


def first_kernel(here_ref, len_ref, k_ref, v_ref, rate_ref, z_ref, ent_ref, own_ref, rates_ref, reach_ref, join_ref):
    spread_rates(rate_ref, rates_ref)
    masks = put_masks(here_ref, len_ref, reach_ref, join_ref, 1)
    for s in range(LB // W):
        at = slice(s * W, (s + 1) * W)
        x = (k_ref[:, at].astype(f32) * v_ref[:, at].astype(f32)).astype(bf16)
        z = swap_blocks([x[m * C : (m + 1) * C] for m in range(NG)])
        for g in range(NG):
            n = s * NG + g
            z_ref[n * C : (n + 1) * C, :] = z[g]
    put_states(z_ref, ent_ref, own_ref, rates_ref[...], masks, 1)


def table_kernel(tapf_ref, tapb_ref, rate_ref, res_ref, lf_ref, lb_ref):
    lane, row = iota(C, 1), iota(C, 0).astype(f32)
    for g in range(LB // G):
        at = slice(g, g + 1)
        rate = jnp.broadcast_to(rate_ref[at, :], (C, W))
        res = jnp.broadcast_to(res_ref[at, :], (C, W))
        for tap_ref, out_ref, lag in ((tapf_ref, lf_ref, row + 1.0), (tapb_ref, lb_ref, C - row)):
            taps = jnp.broadcast_to(tap_ref[at, :], (C, W))
            square = pltpu.roll(taps, 0, 1, stride=1, stride_axis=0)
            carry = res * jnp.exp(-rate * lag)
            hi = carry.astype(bf16).astype(f32)
            carry = jnp.where(lane < C + 2 * R, hi, jnp.where(lane < DEPTH, carry - hi, 0.0))
            out_ref[g * C : (g + 1) * C, :] = jnp.where(lane < C, square, carry).astype(bf16)


def segments(here_ref, len_ref, way):
    first = chunk_places(here_ref, C)
    tokens = docs_at(first + iota(C, 0), len_ref)
    if way > 0:
        return tokens - docs_at(first, len_ref)
    return docs_at(first + (C - 1), len_ref) - tokens


def local_kernel(way, here_ref, len_ref, z_ref, ent_ref, left_ref, y_ref, seg_ref, o_ref):
    @pl.when(pl.program_id(0) == 0)
    def _():
        seg_ref[...] = segments(here_ref, len_ref, way)

    seg = seg_ref[...]
    top = jnp.max(seg)
    m0, m1 = (seg == 0).astype(f32).astype(bf16), (seg == 1).astype(f32).astype(bf16)
    none = jnp.zeros((3 * R, W), bf16)
    for n in range(LB // G):
        entry = ent_ref[n * R : (n + 1) * R, :]
        hi = entry.astype(bf16)
        lo = (entry - hi.astype(f32)).astype(bf16)
        z = z_ref[n * C : (n + 1) * C, :]
        right = jnp.concatenate(
            [jnp.concatenate([z * m0, hi, lo, hi], axis=0), jnp.concatenate([z * m1, none], axis=0)], axis=1
        )
        y = dot(left_ref[n * C : (n + 1) * C, :DEPTH], right)
        o_ref[n] = jnp.where(seg == 0, y[:, :W], y[:, W:]).astype(bf16)

    @pl.when(top > 1)
    def _():
        def again(p, carry):
            mask = (seg == p).astype(f32).astype(bf16)
            for n in range(LB // G):
                square = left_ref[n * C : (n + 1) * C, :C]
                o_ref[n] = jnp.where(seg == p, dot(square, z_ref[n * C : (n + 1) * C, :] * mask), o_ref[n].astype(f32)).astype(bf16)
            return carry

        lax.fori_loop(2, top + 1, again, 0)

    for s in range(LB // W):
        for m, part in enumerate(swap_blocks([o_ref[s * NG + g] for g in range(NG)])):
            y_ref[m * C : (m + 1) * C, s * W : (s + 1) * W] = part


def edge_lags(here_ref, len_ref, flat_ref, s, rows, way):
    start = here_ref[0, 0] * rows
    begin, head, tail = i32(0), i32(1 << 30), i32(0)
    for n in range(DOCS):
        head = jnp.where(begin >= start, jnp.minimum(head, begin), head)
        tail = jnp.where(begin <= start + rows, begin, tail)
        begin += len_ref[n]
    lanes = slice(s * W, (s + 1) * W)
    rate, res = flat_ref[0:1, lanes], flat_ref[1:2, lanes]
    row = iota(C, 0)
    within = row.astype(f32)
    near = res * jnp.exp(-rate * (within + 1.0 if way > 0 else C - within))
    out = []
    for m in range(rows // C):
        token = start + m * C + row
        reached = token < head if way > 0 else token >= tail
        chunks = m if way > 0 else rows // C - 1 - m
        out.append(jnp.where(reached, near * jnp.exp(-rate * (C * chunks)), 0.0).astype(bf16))
    return jnp.concatenate(out, axis=0)


def arrived(here_ref, len_ref, keep_ref, near_ref, far_ref, rates_ref, flat_ref, s, rows, way):
    at = slice(s * W, (s + 1) * W)
    span = jnp.exp(-rates_ref[:, at] * (HOP * rows))
    total = keep_ref[0, 0] * near_ref[:, at].astype(f32) + keep_ref[0, 1] * (span * far_ref[:, at].astype(f32))
    diag = (iota(W, 0) // R) == (iota(W, 1) // G)
    square = jnp.where(diag, jnp.concatenate([total] * NG, axis=0), 0.0)
    hi = square.astype(bf16)
    lo = (square - hi.astype(f32)).astype(bf16)
    lag = edge_lags(here_ref, len_ref, flat_ref, s, rows, way)
    return dot(jnp.concatenate([lag, lag], axis=1), jnp.concatenate([hi, lo], axis=0))


def gate_kernel(
    here_ref, len_ref, keep_ref, near_ref, far_ref, rate_ref, flat_ref, y_ref, q_ref, c_ref, gain_ref,
    conv_ref, stat_ref, acc_ref,
):
    step = pl.program_id(0)
    rows = y_ref.shape[0]

    @pl.when(step == 0)
    def _():
        acc_ref[...] = jnp.zeros_like(acc_ref)

    for s in range(LB // W):
        at = slice(s * W, (s + 1) * W)
        carry = arrived(here_ref, len_ref, keep_ref, near_ref, far_ref, rate_ref, flat_ref, s, rows, 1)
        conv_ref[:, at] = (y_ref[:, at].astype(f32) + carry).astype(bf16)
    for m in range(rows // C):
        part = slice(m * C, (m + 1) * C)
        squares, inner = acc_ref[part, :W], acc_ref[part, W:]
        for s in range(LB // W):
            at = slice(s * W, (s + 1) * W)
            gated = q_ref[part, at].astype(f32) * conv_ref[part, at].astype(f32)
            squares += gated * gated
            inner += c_ref[part, at].astype(f32) * gain_ref[:, at] * gated
        acc_ref[part, :W] = squares
        acc_ref[part, W:] = inner

    @pl.when(step == pl.num_programs(0) - 1)
    def _():
        row = lax.broadcasted_iota(i32, (8, 2 * W), 0)
        lane = lax.broadcasted_iota(i32, (8, 2 * W), 1)
        pick = (row == lane // W).astype(f32)
        stat_ref[...] = lax.dot_general(
            pick, acc_ref[...], (((1,), (1,)), ((), ())), precision=lax.Precision.HIGHEST, preferred_element_type=f32
        )


def grad_kernel(
    total_width, here_ref, len_ref, s0_ref, s1_ref, s2_ref, s3_ref, conv_ref, q_ref, c_ref, gain_ref, rate_ref,
    out_ref, gq_ref, z_ref, ent_ref, own_ref, rates_ref, inv_ref, mean_ref, reach_ref, join_ref,
):
    spread_rates(rate_ref, rates_ref)

    @pl.when(pl.program_id(0) == 0)
    def _():
        stat = s0_ref[...] + s1_ref[...] + s2_ref[...] + s3_ref[...]
        row = iota(8, 0)

        def column(n):
            pick = (row == n).astype(f32)
            return lax.dot_general(
                stat, pick, (((0,), (0,)), ((), ())), precision=lax.Precision.HIGHEST, preferred_element_type=f32
            )

        inv = lax.rsqrt(column(0) / total_width + EPS)
        inv_ref[...] = inv
        mean_ref[...] = inv * column(1) / total_width

    masks = put_masks(here_ref, len_ref, reach_ref, join_ref, -1)
    for s in range(LB // W):
        at = slice(s * W, (s + 1) * W)
        gain = gain_ref[:, at]
        parts = []
        for m in range(NG):
            rows = slice(m * C, (m + 1) * C)
            inv = inv_ref[rows, :]
            q = q_ref[rows, at].astype(f32)
            conv = conv_ref[rows, at].astype(f32)
            normed = q * conv * inv
            out_ref[rows, at] = (normed * gain).astype(bf16)
            grad_gated = inv * (c_ref[rows, at].astype(f32) * gain - normed * mean_ref[rows, :])
            gq_ref[rows, at] = (grad_gated * conv).astype(bf16)
            parts.append((grad_gated * q).astype(bf16))
        z = swap_blocks(parts)
        for g in range(NG):
            n = s * NG + g
            z_ref[n * C : (n + 1) * C, :] = z[g]
    put_states(z_ref, ent_ref, own_ref, rates_ref[...], masks, -1)


def last_kernel(here_ref, len_ref, keep_ref, near_ref, far_ref, rate_ref, flat_ref, y_ref, k_ref, v_ref, gk_ref, gv_ref):
    rows = y_ref.shape[0]
    for s in range(LB // W):
        at = slice(s * W, (s + 1) * W)
        carry = arrived(here_ref, len_ref, keep_ref, near_ref, far_ref, rate_ref, flat_ref, s, rows, -1)
        grad = y_ref[:, at].astype(f32) + carry
        gk_ref[:, at] = (grad * v_ref[:, at].astype(f32)).astype(bf16)
        gv_ref[:, at] = (grad * k_ref[:, at].astype(f32)).astype(bf16)


def doc_index(places, doc_lengths):
    doc_ends = jnp.cumsum(doc_lengths)
    doc_starts = doc_ends - doc_lengths
    return jnp.sum((doc_starts[None, :] <= places[:, None]).astype(i32), axis=1) - 1


def local(query_gate, key_branch, value_branch, norm_gain, residues, decay_rate, doc_lengths, cotangent):
    rows, width = query_gate.shape
    groups = residues.shape[0]
    devices = lax.axis_size("seq")
    here = lax.axis_index("seq")
    total_width = width * lax.axis_size("ch")
    here_arr = here.astype(i32).reshape(1, 1)

    offset = jnp.arange(REACH // rows + 1, dtype=i32)
    docs = doc_index(jnp.concatenate([(here - offset + 1) * rows - 1, (here + offset) * rows]), doc_lengths)
    ends, begins = docs[: len(offset)], docs[len(offset) :]

    def keep(edge, from_, to, way):
        inside = here >= to if way > 0 else here + to < devices
        return ((edge[from_] == edge[to]) & inside).astype(f32)

    keep_f = jnp.stack([keep(ends, 1, 1, 1), keep(ends, 1, 1 + HOP, 1)]).reshape(1, 2)
    keep_b = jnp.stack([keep(begins, 1, 1, -1), keep(begins, 1, 1 + HOP, -1)]).reshape(1, 2)

    rates = jnp.repeat(decay_rate.T, G, axis=1)
    lane = jnp.arange(W)

    def taps(lags):
        h = jnp.sum(residues[:, :, None] * jnp.exp(-decay_rate[:, :, None] * lags.astype(f32)), axis=1)
        return jnp.where(lags < C, h, 0.0)

    tap_f, tap_b = taps((W - lane) % W), taps(lane)
    rate_rep, res_rep = jnp.tile(decay_rate, (1, NG)), jnp.tile(residues, (1, NG))
    flat = jnp.stack([decay_rate.reshape(groups * R), residues.reshape(groups * R)])
    gain = norm_gain.reshape(1, width)

    grid = (width // LB,)
    wide = pl.BlockSpec((rows, LB), lambda i: (0, i))
    modes = pl.BlockSpec((R, LB), lambda i: (0, i))
    stacked = pl.BlockSpec((LB // G * C, W), lambda i: (i, 0))
    states = pl.BlockSpec((LB // G * R, W), lambda i: (i, 0))
    tapped = pl.BlockSpec((LB // G, W), lambda i: (i, 0))
    row1 = pl.BlockSpec((1, LB), lambda i: (0, i))
    small = pl.BlockSpec(memory_space=pltpu.SMEM)
    params = pltpu.CompilerParams(vmem_limit_bytes=VLIM, dimension_semantics=("arbitrary",))

    def shaped(dtype, *shape):
        return jax.ShapeDtypeStruct(shape, dtype)

    full16 = shaped(bf16, rows, width)
    stack16 = shaped(bf16, groups * C, W)
    entries, ends_shape = shaped(f32, groups * R, W), shaped(bf16, R, width)
    rates_of = pl.BlockSpec((groups, R), lambda i: (0, 0))
    kept = [pltpu.VMEM((C, W), bf16), pltpu.VMEM((4, R, W), f32)]
    flat2 = pl.BlockSpec((2, LB), lambda i: (0, i))
    stat_spec = pl.BlockSpec((8, rows), lambda i: (0, 0))

    def ring(x, axis, by):
        size = lax.axis_size(axis)
        return lax.ppermute(x, axis, [(i, (i + by) % size) for i in range(size)])

    def gather(own, way):
        return [own] + [ring(own, "seq", way * n) for n in range(1, HOP)]

    def pass_on(parts, beside, edge, way):
        parts, beside = lax.optimization_barrier((parts, beside))
        total, scale = 0.0, 1.0
        for n, part in enumerate(parts):
            total += keep(edge, 0, n, way) * scale * part.astype(f32)
            scale *= jnp.exp(-rates * rows)
        total = total.astype(bf16)
        return beside, total, ring(total, "seq", way), ring(total, "seq", way * (1 + HOP))

    def within(z, ent, left, way):
        return pl.pallas_call(
            functools.partial(local_kernel, way), grid=grid, in_specs=[small, small, stacked, states, stacked],
            out_specs=wide, out_shape=full16, scratch_shapes=[pltpu.VMEM((C, W), i32), pltpu.VMEM((LB // G, C, W), bf16)],
            compiler_params=params, name="local",
            cost_estimate=pl.CostEstimate(flops=16 * rows * width, bytes_accessed=14 * rows * width, transcendentals=0),
        )(here_arr, doc_lengths, z, ent, left)

    z_f, ent_f, own_f = pl.pallas_call(
        first_kernel, grid=grid, in_specs=[small, small, wide, wide, rates_of], out_specs=[stacked, states, modes],
        out_shape=[stack16, entries, ends_shape], scratch_shapes=[pltpu.VMEM((R, LB), f32)] + kept,
        compiler_params=params, name="first",
    )(here_arr, doc_lengths, key_branch, value_branch, decay_rate)
    parts_f = gather(own_f, 1)
    left_f, left_b = pl.pallas_call(
        table_kernel, grid=grid, in_specs=[tapped] * 4, out_specs=[stacked] * 2,
        out_shape=[stack16] * 2, compiler_params=params, name="tables",
        cost_estimate=pl.CostEstimate(flops=8 * rows * width, bytes_accessed=12 * rows * width, transcendentals=0),
    )(tap_f, tap_b, rate_rep, res_rep)
    left_f, gathered, near_f, far_f = pass_on(parts_f, left_f, ends, 1)
    ent_f, _ = lax.optimization_barrier((ent_f, gathered))
    y_f = within(z_f, ent_f, left_f, 1)
    conv, stat = pl.pallas_call(
        gate_kernel, grid=grid, in_specs=[small] * 3 + [modes] * 3 + [flat2] + [wide] * 3 + [row1],
        out_specs=[wide, stat_spec], out_shape=[full16, shaped(f32, 8, rows)],
        scratch_shapes=[pltpu.VMEM((rows, 2 * W), f32)], compiler_params=params, name="gate",
    )(here_arr, doc_lengths, keep_f, near_f, far_f, rates, flat, y_f, query_gate, cotangent, gain)
    stats = [stat] + [ring(stat, "ch", n) for n in range(1, 4)]
    layer_out, grad_query, z_b, ent_b, own_b = pl.pallas_call(
        functools.partial(grad_kernel, total_width), grid=grid,
        in_specs=[small, small] + [stat_spec] * 4 + [wide] * 3 + [row1, rates_of],
        out_specs=[wide, wide, stacked, states, modes],
        out_shape=[full16, full16, stack16, entries, ends_shape],
        scratch_shapes=[pltpu.VMEM((R, LB), f32)] + [pltpu.VMEM((rows, W), f32)] * 2 + kept,
        compiler_params=params, name="grad",
    )(here_arr, doc_lengths, *stats, conv, query_gate, cotangent, gain, decay_rate)
    parts_b = gather(own_b, -1)
    left_b, gathered, near_b, far_b = pass_on(parts_b, left_b, begins, -1)
    ent_b, _ = lax.optimization_barrier((ent_b, gathered))
    y_b = within(z_b, ent_b, left_b, -1)
    grad_key, grad_value = pl.pallas_call(
        last_kernel, grid=grid, in_specs=[small] * 3 + [modes] * 3 + [flat2] + [wide] * 3, out_specs=[wide, wide],
        out_shape=[full16, full16], compiler_params=params, name="last",
    )(here_arr, doc_lengths, keep_b, near_b, far_b, rates, flat, y_b, key_branch, value_branch)
    return layer_out, grad_query, grad_key, grad_value


def solution(mesh):
    tokens = P("seq", "ch")
    placed = (tokens, tokens, tokens, P("ch"), P("ch", None), P("ch", None), P(), tokens)
    return jax.shard_map(local, mesh=mesh, in_specs=placed, out_specs=(tokens,) * 4, check_vma=False)
```

```python
import functools

import jax
import jax.numpy as jnp
from jax import lax
from jax.experimental import pallas as pl
from jax.experimental.pallas import tpu as pltpu
from jax.sharding import PartitionSpec as P

C = 64
W = 128
LB = 1024
G = 16
R = 16
NG = W // G
DOCS = 16
REACH = 4096
HOP = 4
DEPTH = C + 3 * R
EPS = 1e-6
f32, bf16, i32 = jnp.float32, jnp.bfloat16, jnp.int32
VLIM = 61 * 1024 * 1024


def dot(a, b):
    return jnp.dot(a, b, preferred_element_type=f32)


def iota(rows, axis):
    return lax.broadcasted_iota(i32, (rows, W), axis)


def turn(x, lanes):
    return pltpu.roll(x, lanes % W, 1)


def swap_blocks(parts):
    parts = [part if m == 0 else turn(part, G * m) for m, part in enumerate(parts)]
    blk = iota(parts[0].shape[0], 1) // G
    bit = 1
    while bit < NG:
        up = (blk & bit).astype(f32).astype(parts[0].dtype) > 0
        parts = [jnp.where(up, parts[(m + bit) % NG], parts[m]) for m in range(NG)]
        bit *= 2
    return [parts[0] if g == 0 else turn(parts[NG - g], -G * g) for g in range(NG)]


def fan_out(x):
    blk = iota(x.shape[0], 1) // G
    parts, bit = [x], NG // 2
    while bit:
        low = (blk & bit) == 0
        parts = [
            y
            for x in parts
            for y in (jnp.where(low, x, turn(x, G * bit)), jnp.where(low, turn(x, -G * bit), x))
        ]
        bit //= 2
    return parts


def docs_at(places, len_ref):
    found, start = jnp.full(places.shape, -1, i32), i32(0)
    for n in range(DOCS):
        found += (places >= start).astype(i32)
        start += len_ref[n]
    return found


def chunk_places(here_ref, rows):
    return here_ref[0, 0] * (C * NG) + (iota(rows, 1) // G) * C


def split3(x):
    high = x.astype(bf16)
    rest = x - high.astype(f32)
    middle = rest.astype(bf16)
    return high, middle, (rest - middle.astype(f32)).astype(bf16)


def spread_rates(rate_ref, rate_out_ref):
    groups = rate_ref.shape[1]
    width = rate_out_ref.shape[1]
    row = lax.broadcasted_iota(i32, (groups, width), 0)
    lane = lax.broadcasted_iota(i32, (groups, width), 1)
    pick = (row == (pl.program_id(0) * width + lane) // G).astype(f32).astype(bf16)
    out = dot(jnp.concatenate(split3(rate_ref[...]), axis=0), pick)
    rate_out_ref[...] = out[:R] + out[R : 2 * R] + out[2 * R :]


def put_masks(here_ref, len_ref, reach_ref, join_ref, way):
    @pl.when(pl.program_id(0) == 0)
    def _():
        reach, joins, into = state_masks(here_ref, len_ref, way)
        reach_ref[...] = reach
        for n, join in enumerate(joins + [into]):
            join_ref[n] = join

    return reach_ref[...], [join_ref[n] for n in range(3)], join_ref[3]


def state_masks(here_ref, len_ref, way):
    blk = iota(R, 1) // G
    base = chunk_places(here_ref, R)
    tokens = docs_at(chunk_places(here_ref, C) + iota(C, 0), len_ref)
    if way > 0:
        end, enter = C - 1, 0
        order = blk
    else:
        end, enter = 0, C - 1
        order = NG - 1 - blk
    ends = docs_at(chunk_places(here_ref, C) + end, len_ref)
    reach = (tokens == ends).astype(f32).astype(bf16)
    own = docs_at(base + end, len_ref)
    joins = []
    for n in (1, 2, 4):
        there = docs_at(base + end - way * n * C, len_ref)
        joins.append(((own == there) & (order >= n)).astype(f32))
    prior = docs_at(base + enter - way, len_ref)
    into = ((docs_at(base + enter, len_ref) == prior) & (order >= 1)).astype(f32)
    return reach, joins, into


def chunk_states(z_ref, rates, masks, way):
    reach, joins, into = masks
    passes = LB // W
    lane = iota(R, 1).astype(f32)
    blk = iota(R, 1) // G
    away = (C - 1.0) - lane if way > 0 else lane
    rows = jnp.concatenate([rates[:, s * W : (s + 1) * W] for s in range(passes)], axis=0)
    spread = fan_out(rows)
    order = [(s, g) for s in range(passes) for g in range(NG)]
    rate = jnp.concatenate([spread[g][s * R : (s + 1) * R] for s, g in order], axis=0)
    fall = jnp.exp(-rate * jnp.concatenate([away] * len(order), axis=0))[:, :C]
    hi = fall.astype(bf16)
    lo = (fall - hi.astype(f32)).astype(bf16)
    states = []
    for n in range(len(order)):
        at = slice(n * R, (n + 1) * R)
        both = dot(jnp.concatenate([hi[at], lo[at]], axis=0), z_ref[n * C : (n + 1) * C, :] * reach)
        states.append(both[:R] + both[R:])
    decay = jnp.exp(-rate * C)
    for n, join in zip((1, 2, 4), joins):
        scales = [decay[k * R : (k + 1) * R] * join for k in range(len(order))]
        states = [x + scale * turn(x, way * n * G) for x, scale in zip(states, scales)]
        decay *= decay
    entries = [into * turn(x, way * G) for x in states]
    end = NG - 1 if way > 0 else 0
    last = []
    for s in range(passes):
        row = jnp.zeros((R, W), f32)
        for g in range(NG):
            row = jnp.where(blk == g, turn(states[s * NG + g], (g - end) * G), row)
        last.append(row)
    return entries, last


def put_states(z_ref, ent_ref, own_ref, rates, masks, way):
    entries, last = chunk_states(z_ref, rates, masks, way)
    for n, entry in enumerate(entries):
        ent_ref[n * R : (n + 1) * R, :] = entry
    for s, row in enumerate(last):
        own_ref[:, s * W : (s + 1) * W] = row.astype(bf16)


def first_kernel(here_ref, len_ref, k_ref, v_ref, rate_ref, z_ref, ent_ref, own_ref, rates_ref, reach_ref, join_ref):
    spread_rates(rate_ref, rates_ref)
    masks = put_masks(here_ref, len_ref, reach_ref, join_ref, 1)
    for s in range(LB // W):
        at = slice(s * W, (s + 1) * W)
        x = (k_ref[:, at].astype(f32) * v_ref[:, at].astype(f32)).astype(bf16)
        z = swap_blocks([x[m * C : (m + 1) * C] for m in range(NG)])
        for g in range(NG):
            n = s * NG + g
            z_ref[n * C : (n + 1) * C, :] = z[g]
    put_states(z_ref, ent_ref, own_ref, rates_ref[...], masks, 1)


def table_kernel(tapf_ref, tapb_ref, rates_ref, ress_ref, lf_ref, lb_ref, rate_ref, res_ref):
    step = pl.program_id(0)

    @pl.when(step == 0)
    def _():
        pick = (iota(R, 0) == iota(R, 1) % R).astype(f32).astype(bf16)
        pick = jnp.concatenate([pick] * 3, axis=0)
        for from_ref, to_ref in ((rates_ref, rate_ref), (ress_ref, res_ref)):
            parts = jnp.concatenate(split3(from_ref[...]), axis=0)
            to_ref[...] = lax.dot_general(parts, pick, (((0,), (0,)), ((), ())), preferred_element_type=f32)

    lane, row = iota(C, 1), iota(C, 0).astype(f32)
    for g in range(LB // G):
        at = slice(g, g + 1)
        mine = pl.ds(step * (LB // G) + g, 1)
        rate = jnp.broadcast_to(rate_ref[mine, :], (C, W))
        res = jnp.broadcast_to(res_ref[mine, :], (C, W))
        for tap_ref, out_ref, lag in ((tapf_ref, lf_ref, row + 1.0), (tapb_ref, lb_ref, C - row)):
            taps = jnp.broadcast_to(tap_ref[at, :], (C, W))
            square = pltpu.roll(taps, 0, 1, stride=1, stride_axis=0)
            carry = res * jnp.exp(-rate * lag)
            hi = carry.astype(bf16).astype(f32)
            carry = jnp.where(lane < C + 2 * R, hi, jnp.where(lane < DEPTH, carry - hi, 0.0))
            out_ref[g * C : (g + 1) * C, :] = jnp.where(lane < C, square, carry).astype(bf16)


def segments(here_ref, len_ref, way):
    first = chunk_places(here_ref, C)
    tokens = docs_at(first + iota(C, 0), len_ref)
    if way > 0:
        return tokens - docs_at(first, len_ref)
    return docs_at(first + (C - 1), len_ref) - tokens


def local_kernel(way, here_ref, len_ref, z_ref, ent_ref, left_ref, y_ref, seg_ref, o_ref):
    @pl.when(pl.program_id(0) == 0)
    def _():
        seg_ref[...] = segments(here_ref, len_ref, way)

    seg = seg_ref[...]
    top = jnp.max(seg)
    m0, m1 = (seg == 0).astype(f32).astype(bf16), (seg == 1).astype(f32).astype(bf16)
    none = jnp.zeros((3 * R, W), bf16)
    for n in range(LB // G):
        entry = ent_ref[n * R : (n + 1) * R, :]
        hi = entry.astype(bf16)
        lo = (entry - hi.astype(f32)).astype(bf16)
        z = z_ref[n * C : (n + 1) * C, :]
        right = jnp.concatenate(
            [jnp.concatenate([z * m0, hi, lo, hi], axis=0), jnp.concatenate([z * m1, none], axis=0)], axis=1
        )
        y = dot(left_ref[n * C : (n + 1) * C, :DEPTH], right)
        o_ref[n] = jnp.where(seg == 0, y[:, :W], y[:, W:]).astype(bf16)

    @pl.when(top > 1)
    def _():
        def again(p, carry):
            mask = (seg == p).astype(f32).astype(bf16)
            for n in range(LB // G):
                square = left_ref[n * C : (n + 1) * C, :C]
                o_ref[n] = jnp.where(seg == p, dot(square, z_ref[n * C : (n + 1) * C, :] * mask), o_ref[n].astype(f32)).astype(bf16)
            return carry

        lax.fori_loop(2, top + 1, again, 0)

    for s in range(LB // W):
        for m, part in enumerate(swap_blocks([o_ref[s * NG + g] for g in range(NG)])):
            y_ref[m * C : (m + 1) * C, s * W : (s + 1) * W] = part


def edge_lags(here_ref, len_ref, flat_ref, s, rows, way):
    start = here_ref[0, 0] * rows
    begin, head, tail = i32(0), i32(1 << 30), i32(0)
    for n in range(DOCS):
        head = jnp.where(begin >= start, jnp.minimum(head, begin), head)
        tail = jnp.where(begin <= start + rows, begin, tail)
        begin += len_ref[n]
    lanes = slice(s * W, (s + 1) * W)
    rate, res = flat_ref[0:1, lanes], flat_ref[1:2, lanes]
    row = iota(C, 0)
    within = row.astype(f32)
    near = res * jnp.exp(-rate * (within + 1.0 if way > 0 else C - within))
    out = []
    for m in range(rows // C):
        token = start + m * C + row
        reached = token < head if way > 0 else token >= tail
        chunks = m if way > 0 else rows // C - 1 - m
        out.append(jnp.where(reached, near * jnp.exp(-rate * (C * chunks)), 0.0).astype(bf16))
    return jnp.concatenate(out, axis=0)


def arrived(here_ref, len_ref, keep_ref, near_ref, far_ref, rates_ref, flat_ref, s, rows, way):
    at = slice(s * W, (s + 1) * W)
    span = jnp.exp(-rates_ref[:, at] * (HOP * rows))
    total = keep_ref[0, 0] * near_ref[:, at].astype(f32) + keep_ref[0, 1] * (span * far_ref[:, at].astype(f32))
    diag = (iota(W, 0) // R) == (iota(W, 1) // G)
    square = jnp.where(diag, jnp.concatenate([total] * NG, axis=0), 0.0)
    hi = square.astype(bf16)
    lo = (square - hi.astype(f32)).astype(bf16)
    lag = edge_lags(here_ref, len_ref, flat_ref, s, rows, way)
    return dot(jnp.concatenate([lag, lag], axis=1), jnp.concatenate([hi, lo], axis=0))


def gate_kernel(
    here_ref, len_ref, keep_ref, near_ref, far_ref, rate_ref, flat_ref, y_ref, q_ref, c_ref, gain_ref,
    conv_ref, stat_ref, acc_ref,
):
    step = pl.program_id(0)
    rows = y_ref.shape[0]

    @pl.when(step == 0)
    def _():
        acc_ref[...] = jnp.zeros_like(acc_ref)

    for s in range(LB // W):
        at = slice(s * W, (s + 1) * W)
        carry = arrived(here_ref, len_ref, keep_ref, near_ref, far_ref, rate_ref, flat_ref, s, rows, 1)
        conv_ref[:, at] = (y_ref[:, at].astype(f32) + carry).astype(bf16)
    for m in range(rows // C):
        part = slice(m * C, (m + 1) * C)
        squares, inner = acc_ref[part, :W], acc_ref[part, W:]
        for s in range(LB // W):
            at = slice(s * W, (s + 1) * W)
            gated = q_ref[part, at].astype(f32) * conv_ref[part, at].astype(f32)
            squares += gated * gated
            inner += c_ref[part, at].astype(f32) * gain_ref[:, at] * gated
        acc_ref[part, :W] = squares
        acc_ref[part, W:] = inner

    @pl.when(step == pl.num_programs(0) - 1)
    def _():
        row = lax.broadcasted_iota(i32, (8, 2 * W), 0)
        lane = lax.broadcasted_iota(i32, (8, 2 * W), 1)
        pick = (row == lane // W).astype(f32)
        stat_ref[...] = lax.dot_general(
            pick, acc_ref[...], (((1,), (1,)), ((), ())), precision=lax.Precision.HIGHEST, preferred_element_type=f32
        )


def grad_kernel(
    total_width, here_ref, len_ref, s0_ref, s1_ref, s2_ref, s3_ref, conv_ref, q_ref, c_ref, gain_ref, rate_ref,
    out_ref, gq_ref, z_ref, ent_ref, own_ref, inv_ref, mean_ref, reach_ref, join_ref,
):
    @pl.when(pl.program_id(0) == 0)
    def _():
        stat = s0_ref[...] + s1_ref[...] + s2_ref[...] + s3_ref[...]
        row = iota(8, 0)

        def column(n):
            pick = (row == n).astype(f32)
            return lax.dot_general(
                stat, pick, (((0,), (0,)), ((), ())), precision=lax.Precision.HIGHEST, preferred_element_type=f32
            )

        inv = lax.rsqrt(column(0) / total_width + EPS)
        inv_ref[...] = inv
        mean_ref[...] = inv * column(1) / total_width

    masks = put_masks(here_ref, len_ref, reach_ref, join_ref, -1)
    for s in range(LB // W):
        at = slice(s * W, (s + 1) * W)
        gain = gain_ref[:, at]
        parts = []
        for m in range(NG):
            rows = slice(m * C, (m + 1) * C)
            inv = inv_ref[rows, :]
            q = q_ref[rows, at].astype(f32)
            conv = conv_ref[rows, at].astype(f32)
            normed = q * conv * inv
            out_ref[rows, at] = (normed * gain).astype(bf16)
            grad_gated = inv * (c_ref[rows, at].astype(f32) * gain - normed * mean_ref[rows, :])
            gq_ref[rows, at] = (grad_gated * conv).astype(bf16)
            parts.append((grad_gated * q).astype(bf16))
        z = swap_blocks(parts)
        for g in range(NG):
            n = s * NG + g
            z_ref[n * C : (n + 1) * C, :] = z[g]
    put_states(z_ref, ent_ref, own_ref, rate_ref[...], masks, -1)


def last_kernel(here_ref, len_ref, keep_ref, near_ref, far_ref, rate_ref, flat_ref, y_ref, k_ref, v_ref, gk_ref, gv_ref):
    rows = y_ref.shape[0]
    for s in range(LB // W):
        at = slice(s * W, (s + 1) * W)
        carry = arrived(here_ref, len_ref, keep_ref, near_ref, far_ref, rate_ref, flat_ref, s, rows, -1)
        grad = y_ref[:, at].astype(f32) + carry
        gk_ref[:, at] = (grad * v_ref[:, at].astype(f32)).astype(bf16)
        gv_ref[:, at] = (grad * k_ref[:, at].astype(f32)).astype(bf16)


def doc_index(places, doc_lengths):
    doc_ends = jnp.cumsum(doc_lengths)
    doc_starts = doc_ends - doc_lengths
    return jnp.sum((doc_starts[None, :] <= places[:, None]).astype(i32), axis=1) - 1


def local(query_gate, key_branch, value_branch, norm_gain, residues, decay_rate, doc_lengths, cotangent):
    rows, width = query_gate.shape
    groups = residues.shape[0]
    devices = lax.axis_size("seq")
    here = lax.axis_index("seq")
    total_width = width * lax.axis_size("ch")
    here_arr = here.astype(i32).reshape(1, 1)

    offset = jnp.arange(REACH // rows + 1, dtype=i32)
    docs = doc_index(jnp.concatenate([(here - offset + 1) * rows - 1, (here + offset) * rows]), doc_lengths)
    ends, begins = docs[: len(offset)], docs[len(offset) :]

    def keep(edge, from_, to, way):
        inside = here >= to if way > 0 else here + to < devices
        return ((edge[from_] == edge[to]) & inside).astype(f32)

    keep_f = jnp.stack([keep(ends, 1, 1, 1), keep(ends, 1, 1 + HOP, 1)]).reshape(1, 2)
    keep_b = jnp.stack([keep(begins, 1, 1, -1), keep(begins, 1, 1 + HOP, -1)]).reshape(1, 2)

    lane = jnp.arange(W)

    def taps(lags):
        h = jnp.sum(residues[:, :, None] * jnp.exp(-decay_rate[:, :, None] * lags.astype(f32)), axis=1)
        return jnp.where(lags < C, h, 0.0)

    tap_f, tap_b = taps((W - lane) % W), taps(lane)
    flat = jnp.stack([decay_rate.reshape(groups * R), residues.reshape(groups * R)])
    gain = norm_gain.reshape(1, width)

    grid = (width // LB,)
    wide = pl.BlockSpec((rows, LB), lambda i: (0, i))
    modes = pl.BlockSpec((R, LB), lambda i: (0, i))
    stacked = pl.BlockSpec((LB // G * C, W), lambda i: (i, 0))
    states = pl.BlockSpec((LB // G * R, W), lambda i: (i, 0))
    tapped = pl.BlockSpec((LB // G, W), lambda i: (i, 0))
    row1 = pl.BlockSpec((1, LB), lambda i: (0, i))
    small = pl.BlockSpec(memory_space=pltpu.SMEM)
    params = pltpu.CompilerParams(vmem_limit_bytes=VLIM, dimension_semantics=("arbitrary",))

    def shaped(dtype, *shape):
        return jax.ShapeDtypeStruct(shape, dtype)

    full16 = shaped(bf16, rows, width)
    stack16 = shaped(bf16, groups * C, W)
    entries, ends_shape = shaped(f32, groups * R, W), shaped(bf16, R, width)
    rates_of = pl.BlockSpec((R, groups), lambda i: (0, 0))
    kept = [pltpu.VMEM((C, W), bf16), pltpu.VMEM((4, R, W), f32)]
    flat2 = pl.BlockSpec((2, LB), lambda i: (0, i))
    stat_spec = pl.BlockSpec((8, rows), lambda i: (0, 0))

    def ring(x, axis, by):
        size = lax.axis_size(axis)
        return lax.ppermute(x, axis, [(i, (i + by) % size) for i in range(size)])

    def gather(own, way):
        return [own] + [ring(own, "seq", way * n) for n in range(1, HOP)]

    def pass_on(parts, beside, edge, way):
        parts, beside = lax.optimization_barrier((parts, beside))
        total, scale = 0.0, 1.0
        for n, part in enumerate(parts):
            total += keep(edge, 0, n, way) * scale * part.astype(f32)
            scale *= jnp.exp(-rates * rows)
        total = total.astype(bf16)
        return beside, total, ring(total, "seq", way), ring(total, "seq", way * (1 + HOP))

    def within(z, ent, left, way):
        return pl.pallas_call(
            functools.partial(local_kernel, way), grid=grid, in_specs=[small, small, stacked, states, stacked],
            out_specs=wide, out_shape=full16, scratch_shapes=[pltpu.VMEM((C, W), i32), pltpu.VMEM((LB // G, C, W), bf16)],
            compiler_params=params, name="local",
            cost_estimate=pl.CostEstimate(flops=16 * rows * width, bytes_accessed=14 * rows * width, transcendentals=0),
        )(here_arr, doc_lengths, z, ent, left)

    z_f, ent_f, own_f, rates = pl.pallas_call(
        first_kernel, grid=grid, in_specs=[small, small, wide, wide, rates_of], out_specs=[stacked, states, modes, modes],
        out_shape=[stack16, entries, ends_shape, shaped(f32, R, width)], scratch_shapes=kept,
        compiler_params=params, name="first",
    )(here_arr, doc_lengths, key_branch, value_branch, decay_rate.T)
    parts_f = gather(own_f, 1)
    left_f, left_b = pl.pallas_call(
        table_kernel, grid=grid, in_specs=[tapped] * 2 + [rates_of] * 2, out_specs=[stacked] * 2,
        out_shape=[stack16] * 2, scratch_shapes=[pltpu.VMEM((groups, W), f32)] * 2, compiler_params=params, name="tables",
        cost_estimate=pl.CostEstimate(flops=8 * rows * width, bytes_accessed=12 * rows * width, transcendentals=0),
    )(tap_f, tap_b, decay_rate.T, residues.T)
    left_f, gathered, near_f, far_f = pass_on(parts_f, left_f, ends, 1)
    ent_f, _ = lax.optimization_barrier((ent_f, gathered))
    y_f = within(z_f, ent_f, left_f, 1)
    conv, stat = pl.pallas_call(
        gate_kernel, grid=grid, in_specs=[small] * 3 + [modes] * 3 + [flat2] + [wide] * 3 + [row1],
        out_specs=[wide, stat_spec], out_shape=[full16, shaped(f32, 8, rows)],
        scratch_shapes=[pltpu.VMEM((rows, 2 * W), f32)], compiler_params=params, name="gate",
    )(here_arr, doc_lengths, keep_f, near_f, far_f, rates, flat, y_f, query_gate, cotangent, gain)
    stats = [stat] + [ring(stat, "ch", n) for n in range(1, 4)]
    layer_out, grad_query, z_b, ent_b, own_b = pl.pallas_call(
        functools.partial(grad_kernel, total_width), grid=grid,
        in_specs=[small, small] + [stat_spec] * 4 + [wide] * 3 + [row1, modes],
        out_specs=[wide, wide, stacked, states, modes],
        out_shape=[full16, full16, stack16, entries, ends_shape],
        scratch_shapes=[pltpu.VMEM((rows, W), f32)] * 2 + kept,
        compiler_params=params, name="grad",
    )(here_arr, doc_lengths, *stats, conv, query_gate, cotangent, gain, rates)
    parts_b = gather(own_b, -1)
    left_b, gathered, near_b, far_b = pass_on(parts_b, left_b, begins, -1)
    ent_b, _ = lax.optimization_barrier((ent_b, gathered))
    y_b = within(z_b, ent_b, left_b, -1)
    grad_key, grad_value = pl.pallas_call(
        last_kernel, grid=grid, in_specs=[small] * 3 + [modes] * 3 + [flat2] + [wide] * 3, out_specs=[wide, wide],
        out_shape=[full16, full16], compiler_params=params, name="last",
    )(here_arr, doc_lengths, keep_b, near_b, far_b, rates, flat, y_b, key_branch, value_branch)
    return layer_out, grad_query, grad_key, grad_value


def solution(mesh):
    tokens = P("seq", "ch")
    placed = (tokens, tokens, tokens, P("ch"), P("ch", None), P("ch", None), P(), tokens)
    return jax.shard_map(local, mesh=mesh, in_specs=placed, out_specs=(tokens,) * 4, check_vma=False)
```

```python
import functools

import jax
import jax.numpy as jnp
from jax import lax
from jax.experimental import pallas as pl
from jax.experimental.pallas import tpu as pltpu
from jax.sharding import PartitionSpec as P

C = 64
W = 128
LB = 1024
G = 16
R = 16
NG = W // G
DOCS = 16
REACH = 4096
HOP = 4
DEPTH = C + 3 * R
EPS = 1e-6
f32, bf16, i32 = jnp.float32, jnp.bfloat16, jnp.int32
VLIM = 61 * 1024 * 1024


def dot(a, b):
    return jnp.dot(a, b, preferred_element_type=f32)


def iota(rows, axis):
    return lax.broadcasted_iota(i32, (rows, W), axis)


def turn(x, lanes):
    return pltpu.roll(x, lanes % W, 1)


def swap_blocks(parts):
    parts = [part if m == 0 else turn(part, G * m) for m, part in enumerate(parts)]
    blk = iota(parts[0].shape[0], 1) // G
    bit = 1
    while bit < NG:
        up = (blk & bit).astype(f32).astype(parts[0].dtype) > 0
        parts = [jnp.where(up, parts[(m + bit) % NG], parts[m]) for m in range(NG)]
        bit *= 2
    return [parts[0] if g == 0 else turn(parts[NG - g], -G * g) for g in range(NG)]


def fan_out(x):
    blk = iota(x.shape[0], 1) // G
    parts, bit = [x], NG // 2
    while bit:
        low = (blk & bit) == 0
        parts = [
            y
            for x in parts
            for y in (jnp.where(low, x, turn(x, G * bit)), jnp.where(low, turn(x, -G * bit), x))
        ]
        bit //= 2
    return parts


def docs_at(places, len_ref):
    found, start = jnp.full(places.shape, -1, i32), i32(0)
    for n in range(DOCS):
        found += (places >= start).astype(i32)
        start += len_ref[n]
    return found


def chunk_places(here_ref, rows):
    return here_ref[0, 0] * (C * NG) + (iota(rows, 1) // G) * C


def split3(x):
    high = x.astype(bf16)
    rest = x - high.astype(f32)
    middle = rest.astype(bf16)
    return high, middle, (rest - middle.astype(f32)).astype(bf16)


def spread_rates(rate_ref, rate_out_ref):
    groups = rate_ref.shape[1]
    width = rate_out_ref.shape[1]
    row = lax.broadcasted_iota(i32, (groups, width), 0)
    lane = lax.broadcasted_iota(i32, (groups, width), 1)
    pick = (row == (pl.program_id(0) * width + lane) // G).astype(f32).astype(bf16)
    out = dot(jnp.concatenate(split3(rate_ref[...]), axis=0), pick)
    rate_out_ref[...] = out[:R] + out[R : 2 * R] + out[2 * R :]


def put_masks(here_ref, len_ref, reach_ref, join_ref, way):
    @pl.when(pl.program_id(0) == 0)
    def _():
        reach, joins, into = state_masks(here_ref, len_ref, way)
        reach_ref[...] = reach
        for n, join in enumerate(joins + [into]):
            join_ref[n] = join

    return reach_ref[...], [join_ref[n] for n in range(3)], join_ref[3]


def state_masks(here_ref, len_ref, way):
    blk = iota(R, 1) // G
    base = chunk_places(here_ref, R)
    tokens = docs_at(chunk_places(here_ref, C) + iota(C, 0), len_ref)
    if way > 0:
        end, enter = C - 1, 0
        order = blk
    else:
        end, enter = 0, C - 1
        order = NG - 1 - blk
    ends = docs_at(chunk_places(here_ref, C) + end, len_ref)
    reach = (tokens == ends).astype(f32).astype(bf16)
    own = docs_at(base + end, len_ref)
    joins = []
    for n in (1, 2, 4):
        there = docs_at(base + end - way * n * C, len_ref)
        joins.append(((own == there) & (order >= n)).astype(f32))
    prior = docs_at(base + enter - way, len_ref)
    into = ((docs_at(base + enter, len_ref) == prior) & (order >= 1)).astype(f32)
    return reach, joins, into


def chunk_states(z_ref, rates, masks, way):
    reach, joins, into = masks
    passes = LB // W
    lane = iota(R, 1).astype(f32)
    blk = iota(R, 1) // G
    away = (C - 1.0) - lane if way > 0 else lane
    rows = jnp.concatenate([rates[:, s * W : (s + 1) * W] for s in range(passes)], axis=0)
    spread = fan_out(rows)
    order = [(s, g) for s in range(passes) for g in range(NG)]
    rate = jnp.concatenate([spread[g][s * R : (s + 1) * R] for s, g in order], axis=0)
    fall = jnp.exp(-rate * jnp.concatenate([away] * len(order), axis=0))[:, :C]
    hi = fall.astype(bf16)
    lo = (fall - hi.astype(f32)).astype(bf16)
    states = []
    for n in range(len(order)):
        at = slice(n * R, (n + 1) * R)
        both = dot(jnp.concatenate([hi[at], lo[at]], axis=0), z_ref[n * C : (n + 1) * C, :] * reach)
        states.append(both[:R] + both[R:])
    decay = jnp.exp(-rate * C)
    for n, join in zip((1, 2, 4), joins):
        scales = [decay[k * R : (k + 1) * R] * join for k in range(len(order))]
        states = [x + scale * turn(x, way * n * G) for x, scale in zip(states, scales)]
        decay *= decay
    entries = [into * turn(x, way * G) for x in states]
    end = NG - 1 if way > 0 else 0
    last = []
    for s in range(passes):
        row = jnp.zeros((R, W), f32)
        for g in range(NG):
            row = jnp.where(blk == g, turn(states[s * NG + g], (g - end) * G), row)
        last.append(row)
    return entries, last


def put_states(z_ref, ent_ref, own_ref, rates, masks, way):
    entries, last = chunk_states(z_ref, rates, masks, way)
    for n, entry in enumerate(entries):
        ent_ref[n * R : (n + 1) * R, :] = entry
    for s, row in enumerate(last):
        own_ref[:, s * W : (s + 1) * W] = row.astype(bf16)


def first_kernel(here_ref, len_ref, k_ref, v_ref, rate_ref, z_ref, ent_ref, own_ref, rates_ref, reach_ref, join_ref):
    spread_rates(rate_ref, rates_ref)
    masks = put_masks(here_ref, len_ref, reach_ref, join_ref, 1)
    for s in range(LB // W):
        at = slice(s * W, (s + 1) * W)
        x = (k_ref[:, at].astype(f32) * v_ref[:, at].astype(f32)).astype(bf16)
        z = swap_blocks([x[m * C : (m + 1) * C] for m in range(NG)])
        for g in range(NG):
            n = s * NG + g
            z_ref[n * C : (n + 1) * C, :] = z[g]
    put_states(z_ref, ent_ref, own_ref, rates_ref[...], masks, 1)


def table_kernel(tapf_ref, tapb_ref, rates_ref, ress_ref, lf_ref, lb_ref, rate_ref, res_ref):
    step = pl.program_id(0)

    @pl.when(step == 0)
    def _():
        pick = (iota(R, 0) == iota(R, 1) % R).astype(f32).astype(bf16)
        pick = jnp.concatenate([pick] * 3, axis=0)
        for from_ref, to_ref in ((rates_ref, rate_ref), (ress_ref, res_ref)):
            parts = jnp.concatenate(split3(from_ref[...]), axis=0)
            to_ref[...] = lax.dot_general(parts, pick, (((0,), (0,)), ((), ())), preferred_element_type=f32)

    lane, row = iota(C, 1), iota(C, 0).astype(f32)
    for g in range(LB // G):
        at = slice(g, g + 1)
        mine = pl.ds(step * (LB // G) + g, 1)
        rate = jnp.broadcast_to(rate_ref[mine, :], (C, W))
        res = jnp.broadcast_to(res_ref[mine, :], (C, W))
        for tap_ref, out_ref, lag in ((tapf_ref, lf_ref, row + 1.0), (tapb_ref, lb_ref, C - row)):
            taps = jnp.broadcast_to(tap_ref[at, :], (C, W))
            square = pltpu.roll(taps, 0, 1, stride=1, stride_axis=0)
            carry = res * jnp.exp(-rate * lag)
            hi = carry.astype(bf16).astype(f32)
            carry = jnp.where(lane < C + 2 * R, hi, jnp.where(lane < DEPTH, carry - hi, 0.0))
            out_ref[g * C : (g + 1) * C, :] = jnp.where(lane < C, square, carry).astype(bf16)


def segments(here_ref, len_ref, way):
    first = chunk_places(here_ref, C)
    tokens = docs_at(first + iota(C, 0), len_ref)
    if way > 0:
        return tokens - docs_at(first, len_ref)
    return docs_at(first + (C - 1), len_ref) - tokens


def local_kernel(way, here_ref, len_ref, z_ref, ent_ref, left_ref, y_ref, seg_ref, o_ref):
    @pl.when(pl.program_id(0) == 0)
    def _():
        seg_ref[...] = segments(here_ref, len_ref, way)

    seg = seg_ref[...]
    top = jnp.max(seg)
    m0, m1 = (seg == 0).astype(f32).astype(bf16), (seg == 1).astype(f32).astype(bf16)
    none = jnp.zeros((3 * R, W), bf16)
    for n in range(LB // G):
        entry = ent_ref[n * R : (n + 1) * R, :]
        hi = entry.astype(bf16)
        lo = (entry - hi.astype(f32)).astype(bf16)
        z = z_ref[n * C : (n + 1) * C, :]
        right = jnp.concatenate(
            [jnp.concatenate([z * m0, hi, lo, hi], axis=0), jnp.concatenate([z * m1, none], axis=0)], axis=1
        )
        y = dot(left_ref[n * C : (n + 1) * C, :DEPTH], right)
        o_ref[n] = jnp.where(seg == 0, y[:, :W], y[:, W:]).astype(bf16)

    @pl.when(top > 1)
    def _():
        def again(p, carry):
            mask = (seg == p).astype(f32).astype(bf16)
            for n in range(LB // G):
                square = left_ref[n * C : (n + 1) * C, :C]
                o_ref[n] = jnp.where(seg == p, dot(square, z_ref[n * C : (n + 1) * C, :] * mask), o_ref[n].astype(f32)).astype(bf16)
            return carry

        lax.fori_loop(2, top + 1, again, 0)

    for s in range(LB // W):
        for m, part in enumerate(swap_blocks([o_ref[s * NG + g] for g in range(NG)])):
            y_ref[m * C : (m + 1) * C, s * W : (s + 1) * W] = part


def edge_lags(here_ref, len_ref, flat_ref, s, rows, way):
    start = here_ref[0, 0] * rows
    begin, head, tail = i32(0), i32(1 << 30), i32(0)
    for n in range(DOCS):
        head = jnp.where(begin >= start, jnp.minimum(head, begin), head)
        tail = jnp.where(begin <= start + rows, begin, tail)
        begin += len_ref[n]
    lanes = slice(s * W, (s + 1) * W)
    rate, res = flat_ref[0:1, lanes], flat_ref[1:2, lanes]
    row = iota(C, 0)
    within = row.astype(f32)
    near = res * jnp.exp(-rate * (within + 1.0 if way > 0 else C - within))
    out = []
    for m in range(rows // C):
        token = start + m * C + row
        reached = token < head if way > 0 else token >= tail
        chunks = m if way > 0 else rows // C - 1 - m
        out.append(jnp.where(reached, near * jnp.exp(-rate * (C * chunks)), 0.0).astype(bf16))
    return jnp.concatenate(out, axis=0)


def document(place, len_ref):
    found, start = i32(-1), i32(0)
    for n in range(DOCS):
        found += jnp.where(place >= start, 1, 0)
        start += len_ref[n]
    return found


def edge_keep(here_ref, len_ref, rows, devices, from_, to, way):
    here = here_ref[0, 0]

    def edge(n):
        return document((here - n + 1) * rows - 1 if way > 0 else (here + n) * rows, len_ref)

    inside = here >= to if way > 0 else here + to < devices
    return jnp.where(inside & (edge(from_) == edge(to)), 1.0, 0.0).astype(f32)


def pass_kernel(way, devices, rows, here_ref, len_ref, rate_ref, own_ref, *refs):
    out_ref = refs[-1]
    total, far = own_ref[...].astype(f32), jnp.exp(-rate_ref[...] * rows)
    scale = far
    for n, ref in enumerate(refs[:-1]):
        total += edge_keep(here_ref, len_ref, rows, devices, 0, n + 1, way) * scale * ref[...].astype(f32)
        scale *= far
    out_ref[...] = total.astype(bf16)


def arrived(here_ref, len_ref, keeps, near_ref, far_ref, rates_ref, flat_ref, s, rows, way):
    at = slice(s * W, (s + 1) * W)
    span = jnp.exp(-rates_ref[:, at] * (HOP * rows))
    total = keeps[0] * near_ref[:, at].astype(f32) + keeps[1] * (span * far_ref[:, at].astype(f32))
    diag = (iota(W, 0) // R) == (iota(W, 1) // G)
    square = jnp.where(diag, jnp.concatenate([total] * NG, axis=0), 0.0)
    hi = square.astype(bf16)
    lo = (square - hi.astype(f32)).astype(bf16)
    lag = edge_lags(here_ref, len_ref, flat_ref, s, rows, way)
    return dot(jnp.concatenate([lag, lag], axis=1), jnp.concatenate([hi, lo], axis=0))


def gate_kernel(
    devices, here_ref, len_ref, near_ref, far_ref, rate_ref, flat_ref, y_ref, q_ref, c_ref, gain_ref,
    conv_ref, stat_ref, acc_ref,
):
    step = pl.program_id(0)
    rows = y_ref.shape[0]

    @pl.when(step == 0)
    def _():
        acc_ref[...] = jnp.zeros_like(acc_ref)

    keeps = [edge_keep(here_ref, len_ref, rows, devices, 1, n, 1) for n in (1, 1 + HOP)]
    for s in range(LB // W):
        at = slice(s * W, (s + 1) * W)
        carry = arrived(here_ref, len_ref, keeps, near_ref, far_ref, rate_ref, flat_ref, s, rows, 1)
        conv_ref[:, at] = (y_ref[:, at].astype(f32) + carry).astype(bf16)
    for m in range(rows // C):
        part = slice(m * C, (m + 1) * C)
        squares, inner = acc_ref[part, :W], acc_ref[part, W:]
        for s in range(LB // W):
            at = slice(s * W, (s + 1) * W)
            gated = q_ref[part, at].astype(f32) * conv_ref[part, at].astype(f32)
            squares += gated * gated
            inner += c_ref[part, at].astype(f32) * gain_ref[:, at] * gated
        acc_ref[part, :W] = squares
        acc_ref[part, W:] = inner

    @pl.when(step == pl.num_programs(0) - 1)
    def _():
        row = lax.broadcasted_iota(i32, (8, 2 * W), 0)
        lane = lax.broadcasted_iota(i32, (8, 2 * W), 1)
        pick = (row == lane // W).astype(f32)
        stat_ref[...] = lax.dot_general(
            pick, acc_ref[...], (((1,), (1,)), ((), ())), precision=lax.Precision.HIGHEST, preferred_element_type=f32
        )


def grad_kernel(
    total_width, here_ref, len_ref, s0_ref, s1_ref, s2_ref, s3_ref, conv_ref, q_ref, c_ref, gain_ref, rate_ref,
    out_ref, gq_ref, z_ref, ent_ref, own_ref, inv_ref, mean_ref, reach_ref, join_ref,
):
    @pl.when(pl.program_id(0) == 0)
    def _():
        stat = s0_ref[...] + s1_ref[...] + s2_ref[...] + s3_ref[...]
        row = iota(8, 0)

        def column(n):
            pick = (row == n).astype(f32)
            return lax.dot_general(
                stat, pick, (((0,), (0,)), ((), ())), precision=lax.Precision.HIGHEST, preferred_element_type=f32
            )

        inv = lax.rsqrt(column(0) / total_width + EPS)
        inv_ref[...] = inv
        mean_ref[...] = inv * column(1) / total_width

    masks = put_masks(here_ref, len_ref, reach_ref, join_ref, -1)
    for s in range(LB // W):
        at = slice(s * W, (s + 1) * W)
        gain = gain_ref[:, at]
        parts = []
        for m in range(NG):
            rows = slice(m * C, (m + 1) * C)
            inv = inv_ref[rows, :]
            q = q_ref[rows, at].astype(f32)
            conv = conv_ref[rows, at].astype(f32)
            normed = q * conv * inv
            out_ref[rows, at] = (normed * gain).astype(bf16)
            grad_gated = inv * (c_ref[rows, at].astype(f32) * gain - normed * mean_ref[rows, :])
            gq_ref[rows, at] = (grad_gated * conv).astype(bf16)
            parts.append((grad_gated * q).astype(bf16))
        z = swap_blocks(parts)
        for g in range(NG):
            n = s * NG + g
            z_ref[n * C : (n + 1) * C, :] = z[g]
    put_states(z_ref, ent_ref, own_ref, rate_ref[...], masks, -1)


def last_kernel(devices, here_ref, len_ref, near_ref, far_ref, rate_ref, flat_ref, y_ref, k_ref, v_ref, gk_ref, gv_ref):
    rows = y_ref.shape[0]
    keeps = [edge_keep(here_ref, len_ref, rows, devices, 1, n, -1) for n in (1, 1 + HOP)]
    for s in range(LB // W):
        at = slice(s * W, (s + 1) * W)
        carry = arrived(here_ref, len_ref, keeps, near_ref, far_ref, rate_ref, flat_ref, s, rows, -1)
        grad = y_ref[:, at].astype(f32) + carry
        gk_ref[:, at] = (grad * v_ref[:, at].astype(f32)).astype(bf16)
        gv_ref[:, at] = (grad * k_ref[:, at].astype(f32)).astype(bf16)


def local(query_gate, key_branch, value_branch, norm_gain, residues, decay_rate, doc_lengths, cotangent):
    rows, width = query_gate.shape
    groups = residues.shape[0]
    devices = lax.axis_size("seq")
    here = lax.axis_index("seq")
    total_width = width * lax.axis_size("ch")
    here_arr = here.astype(i32).reshape(1, 1)

    lane = jnp.arange(W)

    def taps(lags):
        h = jnp.sum(residues[:, :, None] * jnp.exp(-decay_rate[:, :, None] * lags.astype(f32)), axis=1)
        return jnp.where(lags < C, h, 0.0)

    tap_f, tap_b = taps((W - lane) % W), taps(lane)
    flat = jnp.stack([decay_rate.reshape(groups * R), residues.reshape(groups * R)])
    gain = norm_gain.reshape(1, width)

    grid = (width // LB,)
    wide = pl.BlockSpec((rows, LB), lambda i: (0, i))
    modes = pl.BlockSpec((R, LB), lambda i: (0, i))
    stacked = pl.BlockSpec((LB // G * C, W), lambda i: (i, 0))
    states = pl.BlockSpec((LB // G * R, W), lambda i: (i, 0))
    tapped = pl.BlockSpec((LB // G, W), lambda i: (i, 0))
    row1 = pl.BlockSpec((1, LB), lambda i: (0, i))
    small = pl.BlockSpec(memory_space=pltpu.SMEM)
    params = pltpu.CompilerParams(vmem_limit_bytes=VLIM, dimension_semantics=("arbitrary",))

    def shaped(dtype, *shape):
        return jax.ShapeDtypeStruct(shape, dtype)

    full16 = shaped(bf16, rows, width)
    stack16 = shaped(bf16, groups * C, W)
    entries, ends_shape = shaped(f32, groups * R, W), shaped(bf16, R, width)
    rates_of = pl.BlockSpec((R, groups), lambda i: (0, 0))
    kept = [pltpu.VMEM((C, W), bf16), pltpu.VMEM((4, R, W), f32)]
    flat2 = pl.BlockSpec((2, LB), lambda i: (0, i))
    stat_spec = pl.BlockSpec((8, rows), lambda i: (0, 0))

    def ring(x, axis, by):
        size = lax.axis_size(axis)
        return lax.ppermute(x, axis, [(i, (i + by) % size) for i in range(size)])

    def gather(own, way):
        return [own] + [ring(own, "seq", way * n) for n in range(1, HOP)]

    def pass_on(parts, beside, way):
        parts, beside = lax.optimization_barrier((parts, beside))
        whole = pl.BlockSpec(memory_space=pltpu.VMEM)
        total = pl.pallas_call(
            functools.partial(pass_kernel, way, devices, rows), in_specs=[small] * 2 + [whole] * (1 + HOP),
            out_specs=whole, out_shape=ends_shape, name="pass_on",
            compiler_params=pltpu.CompilerParams(vmem_limit_bytes=8 * 1024 * 1024),
        )(here_arr, doc_lengths, rates, *parts)
        return beside, total, ring(total, "seq", way), ring(total, "seq", way * (1 + HOP))

    def within(z, ent, left, way):
        return pl.pallas_call(
            functools.partial(local_kernel, way), grid=grid, in_specs=[small, small, stacked, states, stacked],
            out_specs=wide, out_shape=full16, scratch_shapes=[pltpu.VMEM((C, W), i32), pltpu.VMEM((LB // G, C, W), bf16)],
            compiler_params=params, name="local",
            cost_estimate=pl.CostEstimate(flops=16 * rows * width, bytes_accessed=14 * rows * width, transcendentals=0),
        )(here_arr, doc_lengths, z, ent, left)

    z_f, ent_f, own_f, rates = pl.pallas_call(
        first_kernel, grid=grid, in_specs=[small, small, wide, wide, rates_of], out_specs=[stacked, states, modes, modes],
        out_shape=[stack16, entries, ends_shape, shaped(f32, R, width)], scratch_shapes=kept,
        compiler_params=params, name="first",
    )(here_arr, doc_lengths, key_branch, value_branch, decay_rate.T)
    parts_f = gather(own_f, 1)
    left_f, left_b = pl.pallas_call(
        table_kernel, grid=grid, in_specs=[tapped] * 2 + [rates_of] * 2, out_specs=[stacked] * 2,
        out_shape=[stack16] * 2, scratch_shapes=[pltpu.VMEM((groups, W), f32)] * 2, compiler_params=params, name="tables",
        cost_estimate=pl.CostEstimate(flops=8 * rows * width, bytes_accessed=12 * rows * width, transcendentals=0),
    )(tap_f, tap_b, decay_rate.T, residues.T)
    left_f, gathered, near_f, far_f = pass_on(parts_f, left_f, 1)
    ent_f, _ = lax.optimization_barrier((ent_f, gathered))
    y_f = within(z_f, ent_f, left_f, 1)
    conv, stat = pl.pallas_call(
        functools.partial(gate_kernel, devices), grid=grid, in_specs=[small] * 2 + [modes] * 3 + [flat2] + [wide] * 3 + [row1],
        out_specs=[wide, stat_spec], out_shape=[full16, shaped(f32, 8, rows)],
        scratch_shapes=[pltpu.VMEM((rows, 2 * W), f32)], compiler_params=params, name="gate",
    )(here_arr, doc_lengths, near_f, far_f, rates, flat, y_f, query_gate, cotangent, gain)
    stats = [stat] + [ring(stat, "ch", n) for n in range(1, 4)]
    layer_out, grad_query, z_b, ent_b, own_b = pl.pallas_call(
        functools.partial(grad_kernel, total_width), grid=grid,
        in_specs=[small, small] + [stat_spec] * 4 + [wide] * 3 + [row1, modes],
        out_specs=[wide, wide, stacked, states, modes],
        out_shape=[full16, full16, stack16, entries, ends_shape],
        scratch_shapes=[pltpu.VMEM((rows, W), f32)] * 2 + kept,
        compiler_params=params, name="grad",
    )(here_arr, doc_lengths, *stats, conv, query_gate, cotangent, gain, rates)
    parts_b = gather(own_b, -1)
    left_b, gathered, near_b, far_b = pass_on(parts_b, left_b, -1)
    ent_b, _ = lax.optimization_barrier((ent_b, gathered))
    y_b = within(z_b, ent_b, left_b, -1)
    grad_key, grad_value = pl.pallas_call(
        functools.partial(last_kernel, devices), grid=grid, in_specs=[small] * 2 + [modes] * 3 + [flat2] + [wide] * 3, out_specs=[wide, wide],
        out_shape=[full16, full16], compiler_params=params, name="last",
    )(here_arr, doc_lengths, near_b, far_b, rates, flat, y_b, key_branch, value_branch)
    return layer_out, grad_query, grad_key, grad_value


def solution(mesh):
    tokens = P("seq", "ch")
    placed = (tokens, tokens, tokens, P("ch"), P("ch", None), P("ch", None), P(), tokens)
    return jax.shard_map(local, mesh=mesh, in_specs=placed, out_specs=(tokens,) * 4, check_vma=False)
```

```python
import functools

import jax
import jax.numpy as jnp
from jax import lax
from jax.experimental import pallas as pl
from jax.experimental.pallas import tpu as pltpu
from jax.sharding import PartitionSpec as P

C = 64
W = 128
LB = 1024
G = 16
R = 16
NG = W // G
DOCS = 16
REACH = 4096
HOP = 4
DEPTH = C + 3 * R
EPS = 1e-6
f32, bf16, i32 = jnp.float32, jnp.bfloat16, jnp.int32
VLIM = 56 * 1024 * 1024


def dot(a, b):
    return jnp.dot(a, b, preferred_element_type=f32)


def iota(rows, axis):
    return lax.broadcasted_iota(i32, (rows, W), axis)


def turn(x, lanes):
    return pltpu.roll(x, lanes % W, 1)


def swap_blocks(parts):
    parts = [part if m == 0 else turn(part, G * m) for m, part in enumerate(parts)]
    blk = iota(parts[0].shape[0], 1) // G
    bit = 1
    while bit < NG:
        up = (blk & bit).astype(f32).astype(parts[0].dtype) > 0
        parts = [jnp.where(up, parts[(m + bit) % NG], parts[m]) for m in range(NG)]
        bit *= 2
    return [parts[0] if g == 0 else turn(parts[NG - g], -G * g) for g in range(NG)]


def fan_out(x):
    blk = iota(x.shape[0], 1) // G
    parts, bit = [x], NG // 2
    while bit:
        low = (blk & bit) == 0
        parts = [
            y
            for x in parts
            for y in (jnp.where(low, x, turn(x, G * bit)), jnp.where(low, turn(x, -G * bit), x))
        ]
        bit //= 2
    return parts


def docs_at(places, len_ref):
    found, start = jnp.full(places.shape, -1, i32), i32(0)
    for n in range(DOCS):
        found += (places >= start).astype(i32)
        start += len_ref[n]
    return found


def chunk_places(here_ref, rows):
    return here_ref[0, 0] * (C * NG) + (iota(rows, 1) // G) * C


def split3(x):
    high = x.astype(bf16)
    rest = x - high.astype(f32)
    middle = rest.astype(bf16)
    return high, middle, (rest - middle.astype(f32)).astype(bf16)


def spread_rates(rate_ref, rate_out_ref):
    groups = rate_ref.shape[1]
    width = rate_out_ref.shape[1]
    row = lax.broadcasted_iota(i32, (groups, width), 0)
    lane = lax.broadcasted_iota(i32, (groups, width), 1)
    pick = (row == (pl.program_id(0) * width + lane) // G).astype(f32).astype(bf16)
    out = dot(jnp.concatenate(split3(rate_ref[...]), axis=0), pick)
    rate_out_ref[...] = out[:R] + out[R : 2 * R] + out[2 * R :]


def put_masks(here_ref, len_ref, reach_ref, join_ref, way):
    @pl.when(pl.program_id(0) == 0)
    def _():
        reach, joins, into = state_masks(here_ref, len_ref, way)
        reach_ref[...] = reach
        for n, join in enumerate(joins + [into]):
            join_ref[n] = join

    return reach_ref[...], [join_ref[n] for n in range(3)], join_ref[3]


def state_masks(here_ref, len_ref, way):
    blk = iota(R, 1) // G
    base = chunk_places(here_ref, R)
    tokens = docs_at(chunk_places(here_ref, C) + iota(C, 0), len_ref)
    if way > 0:
        end, enter = C - 1, 0
        order = blk
    else:
        end, enter = 0, C - 1
        order = NG - 1 - blk
    ends = docs_at(chunk_places(here_ref, C) + end, len_ref)
    reach = (tokens == ends).astype(f32).astype(bf16)
    own = docs_at(base + end, len_ref)
    joins = []
    for n in (1, 2, 4):
        there = docs_at(base + end - way * n * C, len_ref)
        joins.append(((own == there) & (order >= n)).astype(f32))
    prior = docs_at(base + enter - way, len_ref)
    into = ((docs_at(base + enter, len_ref) == prior) & (order >= 1)).astype(f32)
    return reach, joins, into


def chunk_states(z_ref, rates, masks, way):
    reach, joins, into = masks
    passes = LB // W
    lane = iota(R, 1).astype(f32)
    blk = iota(R, 1) // G
    away = (C - 1.0) - lane if way > 0 else lane
    rows = jnp.concatenate([rates[:, s * W : (s + 1) * W] for s in range(passes)], axis=0)
    spread = fan_out(rows)
    order = [(s, g) for s in range(passes) for g in range(NG)]
    rate = jnp.concatenate([spread[g][s * R : (s + 1) * R] for s, g in order], axis=0)
    fall = jnp.exp(-rate * jnp.concatenate([away] * len(order), axis=0))[:, :C]
    hi = fall.astype(bf16)
    lo = (fall - hi.astype(f32)).astype(bf16)
    states = []
    for n in range(len(order)):
        at = slice(n * R, (n + 1) * R)
        both = dot(jnp.concatenate([hi[at], lo[at]], axis=0), z_ref[n * C : (n + 1) * C, :] * reach)
        states.append(both[:R] + both[R:])
    decay = jnp.exp(-rate * C)
    for n, join in zip((1, 2, 4), joins):
        scales = [decay[k * R : (k + 1) * R] * join for k in range(len(order))]
        states = [x + scale * turn(x, way * n * G) for x, scale in zip(states, scales)]
        decay *= decay
    entries = [into * turn(x, way * G) for x in states]
    end = NG - 1 if way > 0 else 0
    last = []
    for s in range(passes):
        row = jnp.zeros((R, W), f32)
        for g in range(NG):
            row = jnp.where(blk == g, turn(states[s * NG + g], (g - end) * G), row)
        last.append(row)
    return entries, last


def put_states(z_ref, ent_ref, own_ref, rates, masks, way):
    entries, last = chunk_states(z_ref, rates, masks, way)
    for n, entry in enumerate(entries):
        ent_ref[n * R : (n + 1) * R, :] = entry
    for s, row in enumerate(last):
        own_ref[:, s * W : (s + 1) * W] = row.astype(bf16)


def first_kernel(here_ref, len_ref, k_ref, v_ref, rate_ref, z_ref, ent_ref, own_ref, rates_ref, reach_ref, join_ref):
    spread_rates(rate_ref, rates_ref)
    masks = put_masks(here_ref, len_ref, reach_ref, join_ref, 1)
    for s in range(LB // W):
        at = slice(s * W, (s + 1) * W)
        x = (k_ref[:, at].astype(f32) * v_ref[:, at].astype(f32)).astype(bf16)
        z = swap_blocks([x[m * C : (m + 1) * C] for m in range(NG)])
        for g in range(NG):
            n = s * NG + g
            z_ref[n * C : (n + 1) * C, :] = z[g]
    put_states(z_ref, ent_ref, own_ref, rates_ref[...], masks, 1)


def table_kernel(tapf_ref, tapb_ref, rates_ref, ress_ref, lf_ref, lb_ref, rate_ref, res_ref):
    step = pl.program_id(0)

    @pl.when(step == 0)
    def _():
        pick = (iota(R, 0) == iota(R, 1) % R).astype(f32).astype(bf16)
        pick = jnp.concatenate([pick] * 3, axis=0)
        for from_ref, to_ref in ((rates_ref, rate_ref), (ress_ref, res_ref)):
            parts = jnp.concatenate(split3(from_ref[...]), axis=0)
            to_ref[...] = lax.dot_general(parts, pick, (((0,), (0,)), ((), ())), preferred_element_type=f32)

    lane, row = iota(C, 1), iota(C, 0).astype(f32)
    for g in range(LB // G):
        at = slice(g, g + 1)
        mine = pl.ds(step * (LB // G) + g, 1)
        rate = jnp.broadcast_to(rate_ref[mine, :], (C, W))
        res = jnp.broadcast_to(res_ref[mine, :], (C, W))
        for tap_ref, out_ref, lag in ((tapf_ref, lf_ref, row + 1.0), (tapb_ref, lb_ref, C - row)):
            taps = jnp.broadcast_to(tap_ref[at, :], (C, W))
            square = pltpu.roll(taps, 0, 1, stride=1, stride_axis=0)
            carry = res * jnp.exp(-rate * lag)
            hi = carry.astype(bf16).astype(f32)
            carry = jnp.where(lane < C + 2 * R, hi, jnp.where(lane < DEPTH, carry - hi, 0.0))
            out_ref[g * C : (g + 1) * C, :] = jnp.where(lane < C, square, carry).astype(bf16)


def segments(here_ref, len_ref, way):
    first = chunk_places(here_ref, C)
    tokens = docs_at(first + iota(C, 0), len_ref)
    if way > 0:
        return tokens - docs_at(first, len_ref)
    return docs_at(first + (C - 1), len_ref) - tokens


def local_kernel(way, here_ref, len_ref, z_ref, ent_ref, left_ref, y_ref, seg_ref, o_ref):
    @pl.when(pl.program_id(0) == 0)
    def _():
        seg_ref[...] = segments(here_ref, len_ref, way)

    seg = seg_ref[...]
    top = jnp.max(seg)
    m0, m1 = (seg == 0).astype(f32).astype(bf16), (seg == 1).astype(f32).astype(bf16)
    none = jnp.zeros((3 * R, W), bf16)
    for n in range(LB // G):
        entry = ent_ref[n * R : (n + 1) * R, :]
        hi = entry.astype(bf16)
        lo = (entry - hi.astype(f32)).astype(bf16)
        z = z_ref[n * C : (n + 1) * C, :]
        right = jnp.concatenate(
            [jnp.concatenate([z * m0, hi, lo, hi], axis=0), jnp.concatenate([z * m1, none], axis=0)], axis=1
        )
        y = dot(left_ref[n * C : (n + 1) * C, :DEPTH], right)
        o_ref[n] = jnp.where(seg == 0, y[:, :W], y[:, W:]).astype(bf16)

    @pl.when(top > 1)
    def _():
        def again(p, carry):
            mask = (seg == p).astype(f32).astype(bf16)
            for n in range(LB // G):
                square = left_ref[n * C : (n + 1) * C, :C]
                o_ref[n] = jnp.where(seg == p, dot(square, z_ref[n * C : (n + 1) * C, :] * mask), o_ref[n].astype(f32)).astype(bf16)
            return carry

        lax.fori_loop(2, top + 1, again, 0)

    for s in range(LB // W):
        for m, part in enumerate(swap_blocks([o_ref[s * NG + g] for g in range(NG)])):
            y_ref[m * C : (m + 1) * C, s * W : (s + 1) * W] = part


def edge_lags(here_ref, len_ref, flat_ref, s, rows, way):
    start = here_ref[0, 0] * rows
    begin, head, tail = i32(0), i32(1 << 30), i32(0)
    for n in range(DOCS):
        head = jnp.where(begin >= start, jnp.minimum(head, begin), head)
        tail = jnp.where(begin <= start + rows, begin, tail)
        begin += len_ref[n]
    lanes = slice(s * W, (s + 1) * W)
    rate, res = flat_ref[0:1, lanes], flat_ref[1:2, lanes]
    row = iota(C, 0)
    within = row.astype(f32)
    near = res * jnp.exp(-rate * (within + 1.0 if way > 0 else C - within))
    out = []
    for m in range(rows // C):
        token = start + m * C + row
        reached = token < head if way > 0 else token >= tail
        chunks = m if way > 0 else rows // C - 1 - m
        out.append(jnp.where(reached, near * jnp.exp(-rate * (C * chunks)), 0.0).astype(bf16))
    return jnp.concatenate(out, axis=0)


def document(place, len_ref):
    found, start = i32(-1), i32(0)
    for n in range(DOCS):
        found += jnp.where(place >= start, 1, 0)
        start += len_ref[n]
    return found


def edge_keep(here_ref, len_ref, rows, devices, from_, to, way):
    here = here_ref[0, 0]

    def edge(n):
        return document((here - n + 1) * rows - 1 if way > 0 else (here + n) * rows, len_ref)

    inside = here >= to if way > 0 else here + to < devices
    return jnp.where(inside & (edge(from_) == edge(to)), 1.0, 0.0).astype(f32)


def pass_kernel(way, devices, rows, here_ref, len_ref, rate_ref, own_ref, *refs):
    out_ref = refs[-1]
    total, far = own_ref[...].astype(f32), jnp.exp(-rate_ref[...] * rows)
    scale = far
    for n, ref in enumerate(refs[:-1]):
        total += edge_keep(here_ref, len_ref, rows, devices, 0, n + 1, way) * scale * ref[...].astype(f32)
        scale *= far
    out_ref[...] = total.astype(bf16)


def arrived(here_ref, len_ref, keeps, near_ref, far_ref, rates_ref, flat_ref, s, rows, way):
    at = slice(s * W, (s + 1) * W)
    span = jnp.exp(-rates_ref[:, at] * (HOP * rows))
    total = keeps[0] * near_ref[:, at].astype(f32) + keeps[1] * (span * far_ref[:, at].astype(f32))
    diag = (iota(W, 0) // R) == (iota(W, 1) // G)
    square = jnp.where(diag, jnp.concatenate([total] * NG, axis=0), 0.0)
    hi = square.astype(bf16)
    lo = (square - hi.astype(f32)).astype(bf16)
    lag = edge_lags(here_ref, len_ref, flat_ref, s, rows, way)
    return dot(jnp.concatenate([lag, lag], axis=1), jnp.concatenate([hi, lo], axis=0))


def gate_kernel(
    devices, here_ref, len_ref, near_ref, far_ref, rate_ref, flat_ref, y_ref, q_ref, c_ref, gain_ref,
    conv_ref, stat_ref, acc_ref,
):
    step = pl.program_id(0)
    rows = y_ref.shape[0]

    @pl.when(step == 0)
    def _():
        acc_ref[...] = jnp.zeros_like(acc_ref)

    keeps = [edge_keep(here_ref, len_ref, rows, devices, 1, n, 1) for n in (1, 1 + HOP)]
    for s in range(LB // W):
        at = slice(s * W, (s + 1) * W)
        carry = arrived(here_ref, len_ref, keeps, near_ref, far_ref, rate_ref, flat_ref, s, rows, 1)
        conv_ref[:, at] = (y_ref[:, at].astype(f32) + carry).astype(bf16)
    for m in range(rows // C):
        part = slice(m * C, (m + 1) * C)
        squares, inner = acc_ref[part, :W], acc_ref[part, W:]
        for s in range(LB // W):
            at = slice(s * W, (s + 1) * W)
            gated = q_ref[part, at].astype(f32) * conv_ref[part, at].astype(f32)
            squares += gated * gated
            inner += c_ref[part, at].astype(f32) * gain_ref[:, at] * gated
        acc_ref[part, :W] = squares
        acc_ref[part, W:] = inner

    @pl.when(step == pl.num_programs(0) - 1)
    def _():
        row = lax.broadcasted_iota(i32, (8, 2 * W), 0)
        lane = lax.broadcasted_iota(i32, (8, 2 * W), 1)
        pick = (row == lane // W).astype(f32)
        stat_ref[...] = lax.dot_general(
            pick, acc_ref[...], (((1,), (1,)), ((), ())), precision=lax.Precision.HIGHEST, preferred_element_type=f32
        )


def grad_kernel(
    total_width, here_ref, len_ref, s0_ref, s1_ref, s2_ref, s3_ref, conv_ref, q_ref, c_ref, gain_ref, rate_ref,
    out_ref, gq_ref, z_ref, ent_ref, own_ref, inv_ref, mean_ref, reach_ref, join_ref,
):
    @pl.when(pl.program_id(0) == 0)
    def _():
        stat = s0_ref[...] + s1_ref[...] + s2_ref[...] + s3_ref[...]
        row = iota(8, 0)

        def column(n):
            pick = (row == n).astype(f32)
            return lax.dot_general(
                stat, pick, (((0,), (0,)), ((), ())), precision=lax.Precision.HIGHEST, preferred_element_type=f32
            )

        inv = lax.rsqrt(column(0) / total_width + EPS)
        inv_ref[...] = inv
        mean_ref[...] = inv * column(1) / total_width

    masks = put_masks(here_ref, len_ref, reach_ref, join_ref, -1)
    for s in range(LB // W):
        at = slice(s * W, (s + 1) * W)
        gain = gain_ref[:, at]
        parts = []
        for m in range(NG):
            rows = slice(m * C, (m + 1) * C)
            inv = inv_ref[rows, :]
            q = q_ref[rows, at].astype(f32)
            conv = conv_ref[rows, at].astype(f32)
            normed = q * conv * inv
            out_ref[rows, at] = (normed * gain).astype(bf16)
            grad_gated = inv * (c_ref[rows, at].astype(f32) * gain - normed * mean_ref[rows, :])
            gq_ref[rows, at] = (grad_gated * conv).astype(bf16)
            parts.append((grad_gated * q).astype(bf16))
        z = swap_blocks(parts)
        for g in range(NG):
            n = s * NG + g
            z_ref[n * C : (n + 1) * C, :] = z[g]
    put_states(z_ref, ent_ref, own_ref, rate_ref[...], masks, -1)


def last_kernel(devices, here_ref, len_ref, near_ref, far_ref, rate_ref, flat_ref, y_ref, k_ref, v_ref, gk_ref, gv_ref):
    rows = y_ref.shape[0]
    keeps = [edge_keep(here_ref, len_ref, rows, devices, 1, n, -1) for n in (1, 1 + HOP)]
    for s in range(LB // W):
        at = slice(s * W, (s + 1) * W)
        carry = arrived(here_ref, len_ref, keeps, near_ref, far_ref, rate_ref, flat_ref, s, rows, -1)
        grad = y_ref[:, at].astype(f32) + carry
        gk_ref[:, at] = (grad * v_ref[:, at].astype(f32)).astype(bf16)
        gv_ref[:, at] = (grad * k_ref[:, at].astype(f32)).astype(bf16)


def local(query_gate, key_branch, value_branch, norm_gain, residues, decay_rate, doc_lengths, cotangent):
    rows, width = query_gate.shape
    groups = residues.shape[0]
    devices = lax.axis_size("seq")
    here = lax.axis_index("seq")
    total_width = width * lax.axis_size("ch")
    here_arr = here.astype(i32).reshape(1, 1)

    lane = jnp.arange(W)

    def taps(lags):
        h = jnp.sum(residues[:, :, None] * jnp.exp(-decay_rate[:, :, None] * lags.astype(f32)), axis=1)
        return jnp.where(lags < C, h, 0.0)

    tap_f, tap_b = taps((W - lane) % W), taps(lane)
    flat = jnp.stack([decay_rate.reshape(groups * R), residues.reshape(groups * R)])
    gain = norm_gain.reshape(1, width)

    grid = (width // LB,)
    wide = pl.BlockSpec((rows, LB), lambda i: (0, i))
    modes = pl.BlockSpec((R, LB), lambda i: (0, i))
    stacked = pl.BlockSpec((LB // G * C, W), lambda i: (i, 0))
    states = pl.BlockSpec((LB // G * R, W), lambda i: (i, 0))
    tapped = pl.BlockSpec((LB // G, W), lambda i: (i, 0))
    row1 = pl.BlockSpec((1, LB), lambda i: (0, i))
    small = pl.BlockSpec(memory_space=pltpu.SMEM)
    params = pltpu.CompilerParams(vmem_limit_bytes=VLIM, dimension_semantics=("arbitrary",))

    def shaped(dtype, *shape):
        return jax.ShapeDtypeStruct(shape, dtype)

    full16 = shaped(bf16, rows, width)
    stack16 = shaped(bf16, groups * C, W)
    entries, ends_shape = shaped(f32, groups * R, W), shaped(bf16, R, width)
    rates_of = pl.BlockSpec((R, groups), lambda i: (0, 0))
    kept = [pltpu.VMEM((C, W), bf16), pltpu.VMEM((4, R, W), f32)]
    flat2 = pl.BlockSpec((2, LB), lambda i: (0, i))
    stat_spec = pl.BlockSpec((8, rows), lambda i: (0, 0))

    def ring(x, axis, by):
        size = lax.axis_size(axis)
        return lax.ppermute(x, axis, [(i, (i + by) % size) for i in range(size)])

    def gather(own, way):
        return [own] + [ring(own, "seq", way * n) for n in range(1, HOP)]

    def pass_on(parts, beside, way):
        parts, beside = lax.optimization_barrier((parts, beside))
        whole = pl.BlockSpec(memory_space=pltpu.VMEM)
        total = pl.pallas_call(
            functools.partial(pass_kernel, way, devices, rows), in_specs=[small] * 2 + [whole] * (1 + HOP),
            out_specs=whole, out_shape=ends_shape, name="pass_on",
            compiler_params=pltpu.CompilerParams(vmem_limit_bytes=8 * 1024 * 1024),
        )(here_arr, doc_lengths, rates, *parts)
        return beside, total, ring(total, "seq", way), ring(total, "seq", way * (1 + HOP))

    def within(z, ent, left, way):
        return pl.pallas_call(
            functools.partial(local_kernel, way), grid=grid, in_specs=[small, small, stacked, states, stacked],
            out_specs=wide, out_shape=full16, scratch_shapes=[pltpu.VMEM((C, W), i32), pltpu.VMEM((LB // G, C, W), bf16)],
            compiler_params=params, name="local",
            cost_estimate=pl.CostEstimate(flops=16 * rows * width, bytes_accessed=14 * rows * width, transcendentals=0),
        )(here_arr, doc_lengths, z, ent, left)

    z_f, ent_f, own_f, rates = pl.pallas_call(
        first_kernel, grid=grid, in_specs=[small, small, wide, wide, rates_of], out_specs=[stacked, states, modes, modes],
        out_shape=[stack16, entries, ends_shape, shaped(f32, R, width)], scratch_shapes=kept,
        compiler_params=params, name="first",
    )(here_arr, doc_lengths, key_branch, value_branch, decay_rate.T)
    parts_f = gather(own_f, 1)
    left_f, left_b = pl.pallas_call(
        table_kernel, grid=grid, in_specs=[tapped] * 2 + [rates_of] * 2, out_specs=[stacked] * 2,
        out_shape=[stack16] * 2, scratch_shapes=[pltpu.VMEM((groups, W), f32)] * 2, compiler_params=params, name="tables",
        cost_estimate=pl.CostEstimate(flops=8 * rows * width, bytes_accessed=12 * rows * width, transcendentals=0),
    )(tap_f, tap_b, decay_rate.T, residues.T)
    left_f, gathered, near_f, far_f = pass_on(parts_f, left_f, 1)
    ent_f, _ = lax.optimization_barrier((ent_f, gathered))
    y_f = within(z_f, ent_f, left_f, 1)
    conv, stat = pl.pallas_call(
        functools.partial(gate_kernel, devices), grid=grid, in_specs=[small] * 2 + [modes] * 3 + [flat2] + [wide] * 3 + [row1],
        out_specs=[wide, stat_spec], out_shape=[full16, shaped(f32, 8, rows)],
        scratch_shapes=[pltpu.VMEM((rows, 2 * W), f32)], compiler_params=params, name="gate",
    )(here_arr, doc_lengths, near_f, far_f, rates, flat, y_f, query_gate, cotangent, gain)
    stats = [stat] + [ring(stat, "ch", n) for n in range(1, 4)]
    layer_out, grad_query, z_b, ent_b, own_b = pl.pallas_call(
        functools.partial(grad_kernel, total_width), grid=grid,
        in_specs=[small, small] + [stat_spec] * 4 + [wide] * 3 + [row1, modes],
        out_specs=[wide, wide, stacked, states, modes],
        out_shape=[full16, full16, stack16, entries, ends_shape],
        scratch_shapes=[pltpu.VMEM((rows, W), f32)] * 2 + kept,
        compiler_params=params, name="grad",
    )(here_arr, doc_lengths, *stats, conv, query_gate, cotangent, gain, rates)
    parts_b = gather(own_b, -1)
    left_b, gathered, near_b, far_b = pass_on(parts_b, left_b, -1)
    ent_b, _ = lax.optimization_barrier((ent_b, gathered))
    y_b = within(z_b, ent_b, left_b, -1)
    grad_key, grad_value = pl.pallas_call(
        functools.partial(last_kernel, devices), grid=grid, in_specs=[small] * 2 + [modes] * 3 + [flat2] + [wide] * 3, out_specs=[wide, wide],
        out_shape=[full16, full16], compiler_params=params, name="last",
    )(here_arr, doc_lengths, near_b, far_b, rates, flat, y_b, key_branch, value_branch)
    return layer_out, grad_query, grad_key, grad_value


def solution(mesh):
    tokens = P("seq", "ch")
    placed = (tokens, tokens, tokens, P("ch"), P("ch", None), P("ch", None), P(), tokens)
    return jax.shard_map(local, mesh=mesh, in_specs=placed, out_specs=(tokens,) * 4, check_vma=False)
```
